256 devices in a mesh: angle: 16 (over z, core), tile: 4 (over x), cuts: 4 (over y).
Axes of the slice: x: 4, y: 4, z: 8, core: 2. Of those that a mesh axis runs over, the one named last changes fastest.
Arguments:
- objects: float32 [16, 2, 512, 512], P('angle', None, ('tile', 'cuts')), may hold values from -6 to 6
- illumination: float32 [2, 128, 128], replicated, may hold values from -6 to 6
- positions: int32 [16, 256, 2], P('angle', ('tile', 'cuts')), may hold values from 0 to 384
- amplitudes: bfloat16 [16, 256, 128, 128], P('angle', ('tile', 'cuts')), may hold values from 0.25 to 2.5
- projector: bfloat16 [8192, 32768], P(None, ('angle', 'cuts')), may hold values from -0.0625 to 0.0625
Outputs:
- new_objects: float32 [16, 2, 512, 512], P('angle', None, ('tile', 'cuts'))
- volume: float32 [512, 32768], P('tile', ('angle', 'cuts'))
The draws below stay inside these ranges and needn't reach their ends.
All inputs are finite; a program needn't handle non-finite values.
Results may differ from the reference program's by a relative error of at most 0.02.
Values may be sent and summed in bfloat16 or wider, within the bound.
A program may use at most 64 MiB of HBM per device.

```python
import jax
import jax.numpy as jnp
from jax import lax

NPIX = 512
PSIZE = 128
PATCH_DEV = 16
ANGLES = 16
PATCHES = 256
VOXELS = 32768
N_TILE = 4
N_CUTS = 4


def plant(drawn, own_key, smallest, largest):
    longest = drawn.shape.index(max(drawn.shape))
    spots = []
    for shift in (0, 1):
        where = [jax.random.randint(jax.random.fold_in(own_key, axis), (), 0, length) for axis, length in enumerate(drawn.shape)]
        where[longest] = (where[longest] + shift) % drawn.shape[longest]
        spots.append(tuple(where))
    return drawn.at[spots[0]].set(smallest).at[spots[1]].set(largest)


def block_levels(rng, shape, split, smallest, high):
    def one(position, blocks):
        draws = jax.random.uniform(jax.random.fold_in(jax.random.fold_in(rng, 6), position), (blocks,), jnp.float32, smallest / len(split), high / len(split))
        return jnp.repeat(jnp.exp(draws), shape[position] // blocks).reshape((-1,) + (1,) * (len(shape) - position - 1))

    loudness = one(*split[0])
    for cut in split[1:]:
        loudness = loudness * one(*cut)
    return loudness


def scatter_about(own_key, shape, width, bound, shards=(), kind=jnp.bfloat16):
    drawn = jax.random.normal(own_key, shape, jnp.float32) * width
    if len(shards) > 0:
        drawn = block_levels(own_key, shape, shards, -0.22, 0.18) * drawn
    return jnp.clip(drawn, min=-bound, max=bound).astype(kind)


def setup_inputs(seed: int = 0) -> dict:
    key_list = jax.random.split(jax.random.key(seed), 6)
    objects = scatter_about(key_list[0], (ANGLES, 2, NPIX, NPIX), 1.0, 6.0, ((0, 16), (2, 16)), jnp.float32)
    illumination = scatter_about(key_list[1], (2, PSIZE, PSIZE), 1.0, 6.0, (), jnp.float32)
    positions = plant(jax.random.randint(key_list[2], (ANGLES, PATCHES, 2), 0, NPIX - PSIZE + 1), jax.random.fold_in(key_list[2], 1), 0, NPIX - PSIZE).astype(jnp.int32)
    amplitudes = jnp.clip(0.25 + 2.25 * jax.random.uniform(key_list[3], (ANGLES, PATCHES, PSIZE, PSIZE), jnp.float32) ** block_levels(key_list[3], (ANGLES, PATCHES, PSIZE, PSIZE), ((0, 16), (1, 16)), -0.2, 0.2), 0.25, 2.5).astype(jnp.bfloat16)
    projector = scatter_about(key_list[4], (ANGLES * NPIX, VOXELS), (ANGLES * NPIX) ** -0.5, 0.0625, ((1, 64),))
    return dict(objects=objects, illumination=illumination, positions=positions, amplitudes=amplitudes, projector=projector)


step_size = 0.1

def dft_tables(patch_width):
    grid_index = jnp.arange(patch_width, dtype=jnp.int32)
    product_mod = grid_index[:, None] * grid_index[None, :] % patch_width
    phase_table = product_mod.astype(jnp.float32) * (2.0 * jnp.pi / patch_width)
    norm_scale = 1.0 / jnp.sqrt(jnp.float32(patch_width))
    table_real = (jnp.cos(phase_table) * norm_scale).astype(jnp.bfloat16)
    table_imag = (-jnp.sin(phase_table) * norm_scale).astype(jnp.bfloat16)
    table_wide = jnp.concatenate([table_real, table_imag], axis=1)
    table_tall = jnp.concatenate([table_real, table_imag], axis=0)
    return (table_wide, table_tall)

def right_product(stacked, table_wide, conjugate):
    edge_width = stacked.shape[-1]
    result = jnp.einsum('ncij,jk->ncik', stacked.astype(jnp.float32), table_wide.astype(jnp.float32), precision=lax.Precision.HIGHEST)
    from_real = result[:, 0]
    from_imag = result[:, 1]
    if conjugate:
        real_part = from_real[..., :edge_width] + from_imag[..., edge_width:]
        imag_part = from_imag[..., :edge_width] - from_real[..., edge_width:]
    else:
        real_part = from_real[..., :edge_width] - from_imag[..., edge_width:]
        imag_part = from_imag[..., :edge_width] + from_real[..., edge_width:]
    return jnp.stack([real_part, imag_part], axis=1)

def left_product(table_tall, stacked, conjugate):
    edge_width = stacked.shape[-1]
    result = jnp.einsum('kj,ncjm->nckm', table_tall.astype(jnp.float32), stacked.astype(jnp.float32), precision=lax.Precision.HIGHEST)
    from_real = result[:, 0]
    from_imag = result[:, 1]
    if conjugate:
        real_part = from_real[:, :edge_width, :] + from_imag[:, edge_width:, :]
        imag_part = from_imag[:, :edge_width, :] - from_real[:, edge_width:, :]
    else:
        real_part = from_real[:, :edge_width, :] - from_imag[:, edge_width:, :]
        imag_part = from_imag[:, :edge_width, :] + from_real[:, edge_width:, :]
    return jnp.stack([real_part, imag_part], axis=1)

def patch_update(object_half, illumination, place_list, amp_block, table_wide, table_tall):
    edge_width = illumination.shape[-1]
    zero_index = jnp.zeros((), jnp.int32)

    def cut_window(row_at, col_at):
        return lax.dynamic_slice(object_half, (zero_index, row_at, col_at), (2, edge_width, edge_width))
    windows = jax.vmap(cut_window)(place_list[:, 0], place_list[:, 1]).astype(jnp.float32)
    probe_real = illumination[0]
    probe_imag = illumination[1]
    exit_real = probe_real * windows[:, 0] - probe_imag * windows[:, 1]
    exit_imag = probe_real * windows[:, 1] + probe_imag * windows[:, 0]
    exit_half = jnp.stack([exit_real, exit_imag], axis=1).astype(jnp.bfloat16)
    spread = right_product(exit_half, table_wide, False).astype(jnp.bfloat16)
    spectrum = left_product(table_tall, spread, False)
    modulus = jnp.sqrt(spectrum[:, 0] * spectrum[:, 0] + spectrum[:, 1] * spectrum[:, 1])
    scaling = amp_block.astype(jnp.float32) / jnp.maximum(modulus, 1.0)
    projected = (spectrum * scaling[:, None]).astype(jnp.bfloat16)
    back_half = right_product(projected, table_wide, True).astype(jnp.bfloat16)
    revised = left_product(table_tall, back_half, True)
    diff_real = revised[:, 0] - exit_real
    diff_imag = revised[:, 1] - exit_imag
    update_real = step_size * (probe_real * diff_real + probe_imag * diff_imag)
    update_imag = step_size * (probe_real * diff_imag - probe_imag * diff_real)
    patch_terms = jnp.stack([update_real, update_imag], axis=1)
    canvas = jnp.zeros(object_half.shape, jnp.float32)

    def place_one(counter, canvas_now):
        row_at = place_list[counter, 0]
        col_at = place_list[counter, 1]
        current = lax.dynamic_slice(canvas_now, (zero_index, row_at, col_at), (2, edge_width, edge_width))
        return lax.dynamic_update_slice(canvas_now, current + patch_terms[counter], (zero_index, row_at, col_at))
    return lax.fori_loop(0, place_list.shape[0], place_one, canvas)

def reference(objects, illumination, positions, amplitudes, projector):
    table_wide, table_tall = dft_tables(PSIZE)
    block_count = N_TILE * N_CUTS

    def per_angle(inputs):
        object_view, place_list, amp_list = inputs
        object_half = object_view.astype(jnp.bfloat16)

        def per_block(block_inputs):
            block_places, amp_block = block_inputs
            return patch_update(object_half, illumination, block_places, amp_block, table_wide, table_tall).astype(jnp.bfloat16)
        partials = lax.map(per_block, (place_list.reshape(block_count, PATCH_DEV, 2), amp_list.reshape(block_count, PATCH_DEV, PSIZE, PSIZE)))
        partials = lax.optimization_barrier(partials)
        summed = lax.optimization_barrier(jnp.sum(partials.astype(jnp.float32), axis=0))
        renewed = object_view + summed
        phase_image = (object_half[1].astype(jnp.float32) + summed[1]).astype(jnp.bfloat16)
        return (renewed, phase_image)
    new_objects, phase_images = lax.map(per_angle, (objects, positions, amplitudes))
    sinogram = jnp.transpose(phase_images, (1, 0, 2)).reshape(NPIX, ANGLES * NPIX)
    volume = jnp.dot(sinogram, projector, preferred_element_type=jnp.float32)
    return (new_objects, volume)
```

```python
import functools

import jax
import jax.numpy as jnp
import numpy as np
from jax import lax
from jax.experimental import pallas as pl
from jax.experimental.pallas import tpu as pltpu
from jax.sharding import PartitionSpec as P

MESH = pl.DeviceIdType.MESH
STEP_SIZE = 0.1
LANES = 128
CORES = 2


def dft_table(width):
    index = np.arange(width)
    phase = (index[:, None] * index[None, :] % width) * (2.0 * np.pi / width)
    scale = 1.0 / np.sqrt(width)
    table = np.concatenate([np.cos(phase) * scale, -np.sin(phase) * scale], axis=1)
    return jnp.asarray(table.astype(np.float32)).astype(jnp.bfloat16)


def plane_offsets(n_tile, n_cuts):
    pairs = [(dt, dc) for dt in range(n_tile) for dc in range(n_cuts) if (dt, dc) != (0, 0)]
    hops = lambda d, n: min(d, n - d)
    return sorted(pairs, key=lambda o: -(hops(o[0], n_tile) + hops(o[1], n_cuts)))


def gather_kernel(n_tile, n_cuts, obj_ref, img_ref, mine, landed, send_sem, recv_sem):
    t, c = lax.axis_index("tile"), lax.axis_index("cuts")
    rows = obj_ref.shape[1]
    offsets = plane_offsets(n_tile, n_cuts)

    def peer(dt, dc):
        return {"tile": lax.rem(t + dt, n_tile), "cuts": lax.rem(c + dc, n_cuts)}

    barrier = pltpu.get_barrier_semaphore()
    for dt, dc in offsets:
        pl.semaphore_signal(barrier, inc=1, device_id=peer(dt, dc), device_id_type=MESH)
    mine[...] = obj_ref[...].astype(jnp.bfloat16)
    pl.semaphore_wait(barrier, len(offsets))

    copies = []
    for i, (dt, dc) in enumerate(offsets):
        copy = pltpu.make_async_remote_copy(
            src_ref=mine,
            dst_ref=landed.at[i],
            send_sem=send_sem.at[i],
            recv_sem=recv_sem.at[i],
            device_id=peer(dt, dc),
            device_id_type=MESH,
        )
        copy.start()
        copies.append(copy)

    def unpack(block, band):
        at = pl.ds(pl.multiple_of(band * rows, rows), rows)
        for part in range(2):
            for j in range(img_ref.shape[1]):
                img_ref[part, j, at, :] = block[part, :, j * LANES : (j + 1) * LANES].astype(
                    jnp.float32
                )

    unpack(mine, t * n_cuts + c)
    for i in reversed(range(len(offsets))):
        dt, dc = offsets[i]
        copies[i].wait_recv()
        band = lax.rem(t + n_tile - dt, n_tile) * n_cuts + lax.rem(c + n_cuts - dc, n_cuts)
        unpack(landed.at[i], band)
    for copy in copies:
        copy.wait_send()


def patch_kernel(pos_ref, img_ref, amp_ref, probe_ref, table_ref, out_ref, canvas, fwd, bwd):
    width = probe_ref.shape[-1]
    strips = img_ref.shape[1]
    f_re, f_im = table_ref[:, :width], table_ref[:, width:]
    fwd[:width, :width] = f_re
    fwd[:width, width:] = f_im
    fwd[width:, :width] = -f_im
    fwd[width:, width:] = f_re
    bwd[:width, :width] = f_re
    bwd[:width, width:] = -f_im
    bwd[width:, :width] = f_im
    bwd[width:, width:] = f_re
    canvas[...] = jnp.zeros_like(canvas)
    lane = lax.broadcasted_iota(jnp.int32, (width, width), 1)

    def dot(a, b):
        return jnp.dot(a, b, preferred_element_type=jnp.float32)

    def quad(a, b, c, d):
        return jnp.concatenate(
            [jnp.concatenate([a, b], axis=1), jnp.concatenate([c, d], axis=1)], axis=0
        )

    def swap(x):
        w = width
        return quad(x[:w, :w], x[w:, :w], x[:w, w:], x[w:, w:])

    def pair(i, carry):
        exits = []
        for k in range(2):
            row, col = pos_ref[2 * i + k, 0], pos_ref[2 * i + k, 1]
            strip, shift = col // LANES, lax.rem(col, LANES)

            def window(part):
                left = img_ref[part, strip, pl.ds(row, width), :]
                right = img_ref[part, jnp.minimum(strip + 1, strips - 1), pl.ds(row, width), :]
                joined = jnp.where(lane >= shift, left, right)
                return pltpu.roll(joined, lax.rem(LANES - shift, LANES), 1)

            w_re, w_im = window(0), window(1)
            p_re, p_im = probe_ref[0], probe_ref[1]
            exits.append((p_re * w_re - p_im * w_im, p_re * w_im + p_im * w_re))
        ex = quad(*exits[0], *exits[1])
        spread = dot(ex.astype(jnp.bfloat16), fwd[...]).astype(jnp.bfloat16)
        spectrum = dot(bwd[...], swap(spread))
        s_re, s_im = spectrum[:width], spectrum[width:]
        amp = jnp.concatenate([amp_ref[2 * i], amp_ref[2 * i + 1]], axis=1).astype(jnp.float32)
        scaling = amp * lax.rsqrt(jnp.maximum(s_re * s_re + s_im * s_im, 1.0))
        projected = jnp.concatenate([s_re * scaling, s_im * scaling], axis=0)
        back = dot(swap(projected.astype(jnp.bfloat16)), bwd[...]).astype(jnp.bfloat16)
        revised = dot(fwd[...], swap(back))
        for k in range(2):
            row, col = pos_ref[2 * i + k, 0], pos_ref[2 * i + k, 1]
            strip, shift = col // LANES, lax.rem(col, LANES)
            cols = slice(k * width, (k + 1) * width)
            d_re = revised[:width, cols] - exits[k][0]
            d_im = revised[width:, cols] - exits[k][1]
            p_re, p_im = probe_ref[0], probe_ref[1]
            u_re = STEP_SIZE * (p_re * d_re + p_im * d_im)
            u_im = STEP_SIZE * (p_re * d_im - p_im * d_re)
            for part, term in ((0, u_re), (1, u_im)):
                turned = pltpu.roll(term, shift, 1)
                at = pl.ds(row, width)
                canvas[part, strip, at, :] += jnp.where(lane >= shift, turned, 0.0)
                canvas[part, strip + 1, at, :] += jnp.where(lane < shift, turned, 0.0)
        return carry

    lax.fori_loop(0, amp_ref.shape[0] // 2, pair, 0)
    for part in range(2):
        for j in range(strips):
            out_ref[part, :, j * LANES : (j + 1) * LANES] = canvas[part, j].astype(jnp.bfloat16)


def finish_kernel(
    n_angle,
    n_tile,
    n_cuts,
    obj_ref,
    part_ref,
    proj_hbm,
    new_ref,
    vol_ref,
    proj,
    landed,
    phase,
    proj_sem,
    sum_send,
    sum_recv,
    z_send,
    z_recv,
    y_send,
    y_recv,
    s_send,
    s_recv,
):
    a, t, c = lax.axis_index("angle"), lax.axis_index("tile"), lax.axis_index("cuts")
    z, core = a // CORES, lax.rem(a, CORES)
    n_z = n_angle // CORES
    rows, pixels = obj_ref.shape[1:]
    offsets = plane_offsets(n_tile, n_cuts)
    z_steps = sorted(range(1, n_z), key=lambda d: min(d, n_z - d))
    y_steps = list(range(1, n_cuts))

    def plane_peer(dt, dc):
        return {"tile": lax.rem(t + dt, n_tile), "cuts": lax.rem(c + dc, n_cuts)}

    def z_peer(dz):
        return {"angle": lax.rem(z + dz, n_z) * CORES + core}

    def y_peer(dc):
        return {"cuts": lax.rem(c + dc, n_cuts)}

    sibling = {"angle": z * CORES + (1 - core)}

    projector_copy = pltpu.make_async_copy(proj_hbm, proj, proj_sem)
    projector_copy.start()

    barrier = pltpu.get_barrier_semaphore()
    greeted = [plane_peer(*o) for o in offsets] + [z_peer(d) for d in z_steps] + [sibling]
    for device in greeted:
        pl.semaphore_signal(barrier, inc=1, device_id=device, device_id_type=MESH)
    pl.semaphore_wait(barrier, len(greeted))

    def remote(src, dst, send_sem, recv_sem, device):
        copy = pltpu.make_async_remote_copy(
            src_ref=src,
            dst_ref=dst,
            send_sem=send_sem,
            recv_sem=recv_sem,
            device_id=device,
            device_id_type=MESH,
        )
        copy.start()
        return copy

    def band_at(band):
        return pl.ds(pl.multiple_of(band * rows, rows), rows)

    sums = {}
    for part in (1, 0):
        for i, (dt, dc) in enumerate(offsets):
            band = lax.rem(t + dt, n_tile) * n_cuts + lax.rem(c + dc, n_cuts)
            sums[part, i] = remote(
                part_ref.at[part, band_at(band), :],
                landed.at[part, i],
                sum_send.at[part, i],
                sum_recv.at[part, i],
                plane_peer(dt, dc),
            )

    def summed(part):
        total = part_ref[part, band_at(t * n_cuts + c), :].astype(jnp.float32)
        for i in range(len(offsets)):
            sums[part, i].wait_recv()
        for i in range(len(offsets)):
            total = total + landed[part, i].astype(jnp.float32)
        return total

    update = summed(1)
    half = obj_ref[1].astype(jnp.bfloat16).astype(jnp.float32)
    phase[a, c] = (half + update).astype(jnp.bfloat16)
    new_ref[1] = obj_ref[1] + update

    sent = []
    z_copies, y_copies, s_copies = {}, {}, {}

    def source(dz, dc):
        return phase.at[lax.rem(z + n_z - dz, n_z) * CORES + core, lax.rem(c + n_cuts - dc, n_cuts)]

    def to_sibling(dz, dc):
        block = source(dz, dc)
        s_copies[dz, dc] = remote(block, block, s_send.at[dz, dc], s_recv.at[dz, dc], sibling)

    def to_cuts(dz):
        block = source(dz, 0)
        for dc in y_steps:
            y_copies[dz, dc] = remote(block, block, y_send.at[dz, dc], y_recv.at[dz, dc], y_peer(dc))

    own = source(0, 0)
    for dz in z_steps:
        z_copies[dz] = remote(own, own, z_send.at[dz], z_recv.at[dz], z_peer(dz))
    to_cuts(0)
    to_sibling(0, 0)
    for dz in z_steps:
        z_copies[dz].wait_recv()
        to_cuts(dz)
        to_sibling(dz, 0)

    update = summed(0)
    new_ref[0] = obj_ref[0] + update

    projector_copy.wait()

    def project(angle, first):
        block = phase[angle].reshape(n_cuts * rows, pixels)
        weights = proj[pl.ds(pl.multiple_of(angle * pixels, pixels), pixels), :]
        term = jnp.dot(block, weights, preferred_element_type=jnp.float32)
        if first:
            vol_ref[...] = term
        else:
            vol_ref[...] += term

    order = [0] + z_steps
    for dz in order:
        for dc in y_steps:
            y_copies[dz, dc].wait_recv()
            to_sibling(dz, dc)
        project(lax.rem(z + n_z - dz, n_z) * CORES + core, dz == 0)
    for dz in order:
        for dc in [0] + y_steps:
            s_copies[dz, dc].wait_recv()
        project(lax.rem(z + n_z - dz, n_z) * CORES + (1 - core), False)

    for group in (sums, z_copies, y_copies, s_copies):
        for copy in group.values():
            copy.wait_send()


def body(objects, illumination, positions, amplitudes, projector):
    n_angle, n_tile, n_cuts = (lax.axis_size(n) for n in ("angle", "tile", "cuts"))
    _, _, rows, pixels = objects.shape
    width = illumination.shape[-1]
    strips = pixels // LANES
    n_peers = n_tile * n_cuts - 1
    vmem = pl.BlockSpec(memory_space=pltpu.VMEM)
    obj = objects[0]

    image = pl.pallas_call(
        functools.partial(gather_kernel, n_tile, n_cuts),
        out_shape=jax.ShapeDtypeStruct((2, strips, pixels, LANES), jnp.float32),
        in_specs=[vmem],
        out_specs=vmem,
        scratch_shapes=[
            pltpu.VMEM((2, rows, pixels), jnp.bfloat16),
            pltpu.VMEM((n_peers, 2, rows, pixels), jnp.bfloat16),
            pltpu.SemaphoreType.DMA((n_peers,)),
            pltpu.SemaphoreType.DMA((n_peers,)),
        ],
        compiler_params=pltpu.CompilerParams(
            collective_id=0, has_side_effects=True, vmem_limit_bytes=32 * 2**20
        ),
        name="gather_image",
    )(obj)

    partial_sum = pl.pallas_call(
        patch_kernel,
        out_shape=jax.ShapeDtypeStruct((2, pixels, pixels), jnp.bfloat16),
        in_specs=[pl.BlockSpec(memory_space=pltpu.SMEM), vmem, vmem, vmem, vmem],
        out_specs=vmem,
        scratch_shapes=[
            pltpu.VMEM((2, strips + 1, pixels, LANES), jnp.float32),
            pltpu.VMEM((2 * width, 2 * width), jnp.bfloat16),
            pltpu.VMEM((2 * width, 2 * width), jnp.bfloat16),
        ],
        compiler_params=pltpu.CompilerParams(vmem_limit_bytes=32 * 2**20),
        name="patch_update",
    )(positions[0], image, amplitudes[0], illumination, dft_table(width))

    n_z = n_angle // CORES
    new_objects, volume = pl.pallas_call(
        functools.partial(finish_kernel, n_angle, n_tile, n_cuts),
        out_shape=(
            jax.ShapeDtypeStruct((2, rows, pixels), jnp.float32),
            jax.ShapeDtypeStruct((n_cuts * rows, projector.shape[1]), jnp.float32),
        ),
        in_specs=[vmem, vmem, pl.BlockSpec(memory_space=pl.ANY)],
        out_specs=(vmem, vmem),
        scratch_shapes=[
            pltpu.VMEM(projector.shape, jnp.bfloat16),
            pltpu.VMEM((2, n_peers, rows, pixels), jnp.bfloat16),
            pltpu.VMEM((n_angle, n_cuts, rows, pixels), jnp.bfloat16),
            pltpu.SemaphoreType.DMA,
            pltpu.SemaphoreType.DMA((2, n_peers)),
            pltpu.SemaphoreType.DMA((2, n_peers)),
            pltpu.SemaphoreType.DMA((n_z,)),
            pltpu.SemaphoreType.DMA((n_z,)),
            pltpu.SemaphoreType.DMA((n_z, n_cuts)),
            pltpu.SemaphoreType.DMA((n_z, n_cuts)),
            pltpu.SemaphoreType.DMA((n_z, n_cuts)),
            pltpu.SemaphoreType.DMA((n_z, n_cuts)),
        ],
        compiler_params=pltpu.CompilerParams(
            collective_id=1, has_side_effects=True, vmem_limit_bytes=32 * 2**20
        ),
        name="sum_and_project",
    )(obj, partial_sum, projector)
    return new_objects[None], volume


def solution(mesh):
    in_specs = (
        P("angle", None, ("tile", "cuts"), None),
        P(),
        P("angle", ("tile", "cuts"), None),
        P("angle", ("tile", "cuts"), None, None),
        P(None, ("angle", "cuts")),
    )
    out_specs = (P("angle", None, ("tile", "cuts"), None), P("tile", ("angle", "cuts")))
    return jax.shard_map(body, mesh=mesh, in_specs=in_specs, out_specs=out_specs, check_vma=False)
```

```python
import functools

import jax
import jax.numpy as jnp
import numpy as np
from jax import lax
from jax.experimental import pallas as pl
from jax.experimental.pallas import tpu as pltpu
from jax.sharding import PartitionSpec as P

MESH = pl.DeviceIdType.MESH
STEP_SIZE = 0.1
LANES = 128
CORES = 2
COPIES = 160
F32, BF16 = jnp.float32, jnp.bfloat16


def dft_table(width):
    index = np.arange(width)
    phase = (index[:, None] * index[None, :] % width) * (2.0 * np.pi / width)
    scale = 1.0 / np.sqrt(width)
    table = np.concatenate([np.cos(phase) * scale, -np.sin(phase) * scale], axis=1)
    return jnp.asarray(table.astype(np.float32)).astype(BF16)


def dot(a, b):
    return jnp.dot(a, b, preferred_element_type=F32)


def quad(a, b, c, d):
    return jnp.concatenate(
        [jnp.concatenate([a, b], axis=1), jnp.concatenate([c, d], axis=1)], axis=0
    )


def swap(x):
    w = x.shape[0] // 2
    return quad(x[:w, :w], x[w:, :w], x[:w, w:], x[w:, w:])


def near_first(n):
    return sorted(range(1, n), key=lambda d: min(d, n - d))


def kernel(
    n_angle,
    n_tile,
    n_cuts,
    pos_ref,
    obj_hbm,
    amp_hbm,
    probe_hbm,
    table_hbm,
    proj_hbm,
    new_ref,
    vol_ref,
    obj,
    amp,
    probe,
    table,
    proj,
    bands,
    image,
    fwd,
    bwd,
    terms,
    canvas,
    first_x,
    first_y,
    slab_sum,
    staged,
    last_x,
    last_y,
    real_first,
    real_sum,
    real_staged,
    real_last,
    phase,
    load_sem,
    send_sem,
    recv_sem,
):
    a, t, c = lax.axis_index("angle"), lax.axis_index("tile"), lax.axis_index("cuts")
    z, core = a // CORES, lax.rem(a, CORES)
    n_z = n_angle // CORES
    rows, pixels = obj.shape[1:]
    width = probe.shape[-1]
    strips = pixels // LANES
    half = pixels // 2
    n_patch = amp.shape[0]
    pad = pixels - width
    x_steps, y_steps, z_steps = near_first(n_tile), near_first(n_cuts), near_first(n_z)

    def ahead(at, step, n):
        return lax.rem(at + step, n)

    def behind(at, step, n):
        return lax.rem(at + n - step, n)

    def x_peer(d):
        return {"tile": ahead(t, d, n_tile)}

    def y_peer(d):
        return {"cuts": ahead(c, d, n_cuts)}

    def z_peer(d):
        return {"angle": ahead(z, d, n_z) * CORES + core}

    sibling = {"angle": z * CORES + (1 - core)}
    sent = []

    def remote(src, dst, device):
        i = len(sent)
        copy = pltpu.make_async_remote_copy(
            src_ref=src,
            dst_ref=dst,
            send_sem=send_sem.at[i],
            recv_sem=recv_sem.at[i],
            device_id=device,
            device_id_type=MESH,
        )
        copy.start()
        sent.append(copy)
        return copy

    loads = [
        pltpu.make_async_copy(src, dst, load_sem.at[i])
        for i, (src, dst) in enumerate(
            [
                (obj_hbm, obj),
                (probe_hbm, probe),
                (table_hbm, table),
                (amp_hbm, amp),
                (proj_hbm, proj),
            ]
        )
    ]
    for load in loads:
        load.start()
    barrier = pltpu.get_barrier_semaphore()
    greeted = [x_peer(d) for d in x_steps] + [y_peer(d) for d in y_steps]
    greeted += [z_peer(d) for d in z_steps] + [sibling]
    for device in greeted:
        pl.semaphore_signal(barrier, inc=1, device_id=device, device_id_type=MESH)
    loads[0].wait()
    for part in range(2):
        bands[part, t, c] = obj[part].astype(BF16)
    pl.semaphore_wait(barrier, len(greeted))

    first, second = {}, {}

    def go_x(part, tt, cc, key):
        for d in x_steps:
            block = bands.at[part, tt, cc]
            key[d] = remote(block, block, x_peer(d))

    def go_y(part, tt, cc, key):
        for d in y_steps:
            block = bands.at[part, tt, cc]
            key[d] = remote(block, block, y_peer(d))

    for part in range(2):
        first[part] = {}
        second[part, 0] = {}
    go_x(0, t, c, first[0])
    go_y(1, t, c, first[1])
    go_y(0, t, c, second[0, 0])
    go_x(1, t, c, second[1, 0])

    terms_zero = jnp.zeros((pad, LANES), F32)

    @pl.loop(0, n_patch)
    def _(p):
        for part in range(2):
            terms[p, part, :pad] = terms_zero
            terms[p, part, pad + width :] = terms_zero

    loads[1].wait()
    loads[2].wait()
    f_re, f_im = table[:, :width], table[:, width:]
    fwd[...] = quad(f_re, f_im, -f_im, f_re)
    bwd[...] = quad(f_re, -f_im, f_im, f_re)

    def unpack(part, tt, cc):
        at = pl.ds(pl.multiple_of((tt * n_cuts + cc) * rows, rows), rows)
        block = bands[part, tt, cc]
        for j in range(strips):
            image[part, j, at, :] = block[:, j * LANES : (j + 1) * LANES].astype(F32)

    unpack(0, t, c)
    unpack(1, t, c)
    for i in range(max(len(x_steps), len(y_steps))):
        if i < len(x_steps):
            d = x_steps[i]
            first[0][d].wait_recv()
            second[0, d] = {}
            go_y(0, behind(t, d, n_tile), c, second[0, d])
        if i < len(y_steps):
            d = y_steps[i]
            first[1][d].wait_recv()
            second[1, d] = {}
            go_x(1, t, behind(c, d, n_cuts), second[1, d])
    for d in x_steps:
        unpack(0, behind(t, d, n_tile), c)
    for d in y_steps:
        unpack(1, t, behind(c, d, n_cuts))
    for d in [0] + x_steps:
        for e in y_steps:
            second[0, d][e].wait_recv()
            unpack(0, behind(t, d, n_tile), behind(c, e, n_cuts))
    for d in [0] + y_steps:
        for e in x_steps:
            second[1, d][e].wait_recv()
            unpack(1, behind(t, e, n_tile), behind(c, d, n_cuts))
    loads[3].wait()

    lane = lax.broadcasted_iota(jnp.int32, (width, LANES), 1)

    def pair(i, carry):
        exits = []
        p_re, p_im = probe[0], probe[1]
        for k in range(2):
            row, col = pos_ref[0, 2 * i + k], pos_ref[1, 2 * i + k]
            strip, shift = col // LANES, lax.rem(col, LANES)

            def window(part):
                left = image[part, strip, pl.ds(row, width), :]
                right = image[part, jnp.minimum(strip + 1, strips - 1), pl.ds(row, width), :]
                joined = jnp.where(lane >= shift, left, right)
                return pltpu.roll(joined, lax.rem(LANES - shift, LANES), 1)

            w_re, w_im = window(0), window(1)
            exits.append((p_re * w_re - p_im * w_im, p_re * w_im + p_im * w_re))
        spread = dot(quad(*exits[0], *exits[1]).astype(BF16), fwd[...]).astype(BF16)
        spectrum = dot(bwd[...], swap(spread))
        s_re, s_im = spectrum[:width], spectrum[width:]
        measured = jnp.concatenate([amp[2 * i], amp[2 * i + 1]], axis=1).astype(F32)
        scaling = measured * lax.rsqrt(jnp.maximum(s_re * s_re + s_im * s_im, 1.0))
        projected = jnp.concatenate([s_re * scaling, s_im * scaling], axis=0).astype(BF16)
        back = dot(swap(projected), bwd[...]).astype(BF16)
        revised = dot(fwd[...], swap(back))
        for k in range(2):
            shift = lax.rem(pos_ref[1, 2 * i + k], LANES)
            cols = slice(k * width, (k + 1) * width)
            d_re = revised[:width, cols] - exits[k][0]
            d_im = revised[width:, cols] - exits[k][1]
            u_re = STEP_SIZE * (p_re * d_re + p_im * d_im)
            u_im = STEP_SIZE * (p_re * d_im - p_im * d_re)
            terms[2 * i + k, 0, pad : pad + width] = pltpu.roll(u_re, shift, 1)
            terms[2 * i + k, 1, pad : pad + width] = pltpu.roll(u_im, shift, 1)
        return carry

    lax.fori_loop(0, n_patch // 2, pair, 0)

    piece = 64
    lane8 = lax.broadcasted_iota(jnp.int32, (8, LANES), 1)

    def build(part, slab):
        for q in range(n_cuts * rows // piece):
            base = pad + slab * (n_cuts * rows) + q * piece

            def add(p, totals):
                row, col = pos_ref[0, p], pos_ref[1, p]
                strip, shift = col // LANES, lax.rem(col, LANES)
                block = terms[p, part, pl.ds(base - row, piece), :].reshape(piece // 8, 8, LANES)
                place = strip + jnp.where(lane8 < shift, 1, 0)
                return tuple(
                    total + jnp.where((place == j)[None], block, 0.0)
                    for j, total in enumerate(totals)
                )

            zero = jnp.zeros((piece // 8, 8, LANES), F32)
            totals = lax.fori_loop(0, n_patch, add, (zero,) * strips, unroll=2)
            for h in range(2):
                wide = jnp.concatenate(
                    [x.reshape(piece, LANES) for x in totals[h * strips // 2 : (h + 1) * strips // 2]],
                    axis=1,
                ).astype(BF16)
                for b in range(piece // rows):
                    canvas[part, h, slab, q * (piece // rows) + b] = wide[b * rows : (b + 1) * rows]

    sum_x, sum_y = {}, {}
    for d in reversed(x_steps):
        slab = ahead(t, d, n_tile)
        build(1, slab)
        sum_x[d] = remote(canvas.at[1, 0, slab], first_x.at[d - 1], x_peer(d))
    build(1, t)
    for d in reversed(y_steps):
        sum_y[d] = remote(canvas.at[1, 1, :, ahead(c, d, n_cuts)], first_y.at[d - 1], y_peer(d))
    for d in reversed(x_steps):
        build(0, ahead(t, d, n_tile))
    build(0, t)

    fin_x, fin_y = {}, {}
    for d in x_steps:
        sum_x[d].wait_recv()
    total = canvas[1, 0, t].astype(F32)
    for d in x_steps:
        total = total + first_x[d - 1].astype(F32)
    slab_sum[0] = total
    staged[0] = total.astype(BF16)
    for d in reversed(y_steps):
        fin_y[d] = remote(staged.at[0, ahead(c, d, n_cuts)], last_y.at[d - 1], y_peer(d))
    for d in y_steps:
        sum_y[d].wait_recv()
    for tt in range(n_tile):
        total = canvas[1, 1, tt, c].astype(F32)
        for d in y_steps:
            total = total + first_y[d - 1, tt].astype(F32)
        slab_sum[1, tt] = total
        staged[1, tt] = total.astype(BF16)
    for d in reversed(x_steps):
        fin_x[d] = remote(staged.at[1, ahead(t, d, n_tile)], last_x.at[d - 1], x_peer(d))
    for d in y_steps:
        fin_y[d].wait_recv()
    left = slab_sum[0, c]
    for d in y_steps:
        left = left + last_y[d - 1].astype(F32)
    for d in x_steps:
        fin_x[d].wait_recv()
    right = slab_sum[1, t]
    for d in x_steps:
        right = right + last_x[d - 1].astype(F32)
    update = jnp.concatenate([left, right], axis=1)
    phase[a, c] = (bands[1, t, c].astype(F32) + update).astype(BF16)
    new_ref[1] = obj[1] + update

    z_copies, y_copies, s_copies = {}, {}, {}

    def block_at(dz, dc):
        return phase.at[behind(z, dz, n_z) * CORES + core, behind(c, dc, n_cuts)]

    def to_sibling(dz, dc):
        block = block_at(dz, dc)
        s_copies[dz, dc] = remote(block, block, sibling)

    def to_cuts(dz):
        block = block_at(dz, 0)
        for dc in y_steps:
            y_copies[dz, dc] = remote(block, block, y_peer(dc))

    own = block_at(0, 0)
    for dz in z_steps:
        z_copies[dz] = remote(own, own, z_peer(dz))
    to_cuts(0)
    to_sibling(0, 0)

    real_x, real_y = {}, {}
    for d in reversed(x_steps):
        real_x[d] = remote(canvas.at[0, :, ahead(t, d, n_tile)], real_first.at[d - 1], x_peer(d))

    for dz in z_steps:
        z_copies[dz].wait_recv()
        to_cuts(dz)
        to_sibling(dz, 0)

    for d in x_steps:
        real_x[d].wait_recv()
    for h in range(2):
        total = canvas[0, h, t].astype(F32)
        for d in x_steps:
            total = total + real_first[d - 1, h].astype(F32)
        real_sum[h] = total
        for cc in range(n_cuts):
            real_staged[cc, h] = total[cc].astype(BF16)
    for d in y_steps:
        real_y[d] = remote(real_staged.at[ahead(c, d, n_cuts)], real_last.at[d - 1], y_peer(d))

    loads[4].wait()

    def project(angle, start):
        block = phase[angle].reshape(n_cuts * rows, pixels)
        weights = proj[pl.ds(pl.multiple_of(angle * pixels, pixels), pixels), :]
        term = dot(block, weights)
        if start:
            vol_ref[...] = term
        else:
            vol_ref[...] += term

    order = [0] + z_steps
    for dz in order:
        for dc in y_steps:
            y_copies[dz, dc].wait_recv()
            to_sibling(dz, dc)
        project(behind(z, dz, n_z) * CORES + core, dz == 0)
    for d in y_steps:
        real_y[d].wait_recv()
    for h in range(2):
        total = real_sum[h, c]
        for d in y_steps:
            total = total + real_last[d - 1, h].astype(F32)
        cols = slice(h * half, (h + 1) * half)
        new_ref[0, :, cols] = obj[0, :, cols] + total
    for dz in order:
        for dc in [0] + y_steps:
            s_copies[dz, dc].wait_recv()
        project(behind(z, dz, n_z) * CORES + (1 - core), False)
    for copy in sent:
        copy.wait_send()


def body(objects, illumination, positions, amplitudes, projector):
    n_angle, n_tile, n_cuts = (lax.axis_size(n) for n in ("angle", "tile", "cuts"))
    _, _, rows, pixels = objects.shape
    n_patch = positions.shape[1]
    width = illumination.shape[-1]
    strips = pixels // LANES
    half = pixels // 2
    pad = pixels - width
    vmem = pl.BlockSpec(memory_space=pltpu.VMEM)
    hbm = pl.BlockSpec(memory_space=pltpu.HBM)

    new_objects, volume = pl.pallas_call(
        functools.partial(kernel, n_angle, n_tile, n_cuts),
        out_shape=(
            jax.ShapeDtypeStruct((2, rows, pixels), F32),
            jax.ShapeDtypeStruct((n_cuts * rows, projector.shape[1]), F32),
        ),
        in_specs=[pl.BlockSpec(memory_space=pltpu.SMEM)] + [hbm] * 5,
        out_specs=(vmem, vmem),
        scratch_shapes=[
            pltpu.VMEM((2, rows, pixels), F32),
            pltpu.VMEM((n_patch, width, width), BF16),
            pltpu.VMEM((2, width, width), F32),
            pltpu.VMEM((width, 2 * width), BF16),
            pltpu.VMEM(projector.shape, BF16),
            pltpu.VMEM((2, n_tile, n_cuts, rows, pixels), BF16),
            pltpu.VMEM((2, strips, pixels, LANES), F32),
            pltpu.VMEM((2 * width, 2 * width), BF16),
            pltpu.VMEM((2 * width, 2 * width), BF16),
            pltpu.VMEM((n_patch, 2, 2 * pad + width, LANES), F32),
            pltpu.VMEM((2, 2, n_tile, n_cuts, rows, half), BF16),
            pltpu.VMEM((n_tile - 1, n_cuts, rows, half), BF16),
            pltpu.VMEM((n_cuts - 1, n_tile, rows, half), BF16),
            pltpu.VMEM((2, n_cuts, rows, half), F32),
            pltpu.VMEM((2, n_cuts, rows, half), BF16),
            pltpu.VMEM((n_tile - 1, rows, half), BF16),
            pltpu.VMEM((n_cuts - 1, rows, half), BF16),
            pltpu.VMEM((n_tile - 1, 2, n_cuts, rows, half), BF16),
            pltpu.VMEM((2, n_cuts, rows, half), F32),
            pltpu.VMEM((n_cuts, 2, rows, half), BF16),
            pltpu.VMEM((n_cuts - 1, 2, rows, half), BF16),
            pltpu.VMEM((n_angle, n_cuts, rows, pixels), BF16),
            pltpu.SemaphoreType.DMA((5,)),
            pltpu.SemaphoreType.DMA((COPIES,)),
            pltpu.SemaphoreType.DMA((COPIES,)),
        ],
        compiler_params=pltpu.CompilerParams(
            collective_id=0, has_side_effects=True, vmem_limit_bytes=56 * 2**20
        ),
        name="update_and_project",
    )(positions[0].T, objects[0], amplitudes[0], illumination, dft_table(width), projector)
    return new_objects[None], volume


def solution(mesh):
    in_specs = (
        P("angle", None, ("tile", "cuts"), None),
        P(),
        P("angle", ("tile", "cuts"), None),
        P("angle", ("tile", "cuts"), None, None),
        P(None, ("angle", "cuts")),
    )
    out_specs = (P("angle", None, ("tile", "cuts"), None), P("tile", ("angle", "cuts")))
    return jax.shard_map(body, mesh=mesh, in_specs=in_specs, out_specs=out_specs, check_vma=False)
```

```python
import functools

import jax
import jax.numpy as jnp
import numpy as np
from jax import lax
from jax.experimental import pallas as pl
from jax.experimental.pallas import tpu as pltpu
from jax.sharding import PartitionSpec as P

MESH = pl.DeviceIdType.MESH
STEP_SIZE = 0.1
LANES = 128
CORES = 2
COPIES = 160
F32, BF16 = jnp.float32, jnp.bfloat16


def dft_table(width):
    index = np.arange(width)
    phase = (index[:, None] * index[None, :] % width) * (2.0 * np.pi / width)
    scale = 1.0 / np.sqrt(width)
    table = np.concatenate([np.cos(phase) * scale, -np.sin(phase) * scale], axis=1)
    return jnp.asarray(table.astype(np.float32)).astype(BF16)


def dot(a, b):
    return jnp.dot(a, b, preferred_element_type=F32)


def quad(a, b, c, d):
    return jnp.concatenate(
        [jnp.concatenate([a, b], axis=1), jnp.concatenate([c, d], axis=1)], axis=0
    )


def swap(x):
    w = x.shape[0] // 2
    return quad(x[:w, :w], x[w:, :w], x[:w, w:], x[w:, w:])


def near_first(n):
    return sorted(range(1, n), key=lambda d: min(d, n - d))


def kernel(
    n_angle,
    n_tile,
    n_cuts,
    pos_hbm,
    obj_hbm,
    amp_hbm,
    probe_hbm,
    table_hbm,
    proj_hbm,
    new_ref,
    vol_ref,
    obj,
    amp,
    probe,
    table,
    proj,
    bands,
    image,
    fwd,
    bwd,
    terms,
    canvas,
    first_x,
    first_y,
    slab_sum,
    staged,
    last_x,
    last_y,
    real_first,
    real_sum,
    real_staged,
    real_last,
    phase,
    pos_ref,
    load_sem,
    send_sem,
    recv_sem,
):
    a, t, c = lax.axis_index("angle"), lax.axis_index("tile"), lax.axis_index("cuts")
    z, core = a // CORES, lax.rem(a, CORES)
    n_z = n_angle // CORES
    rows, pixels = obj.shape[1:]
    width = probe.shape[-1]
    strips = pixels // LANES
    half = pixels // 2
    n_patch = amp.shape[0]
    pad = pixels - width
    x_steps, y_steps, z_steps = near_first(n_tile), near_first(n_cuts), near_first(n_z)

    def ahead(at, step, n):
        return lax.rem(at + step, n)

    def behind(at, step, n):
        return lax.rem(at + n - step, n)

    def x_peer(d):
        return {"tile": ahead(t, d, n_tile)}

    def y_peer(d):
        return {"cuts": ahead(c, d, n_cuts)}

    def z_peer(d):
        return {"angle": ahead(z, d, n_z) * CORES + core}

    sibling = {"angle": z * CORES + (1 - core)}
    sent = []

    def remote(src, dst, device):
        i = len(sent)
        copy = pltpu.make_async_remote_copy(
            src_ref=src,
            dst_ref=dst,
            send_sem=send_sem.at[i],
            recv_sem=recv_sem.at[i],
            device_id=device,
            device_id_type=MESH,
        )
        copy.start()
        sent.append(copy)
        return copy

    loads = [
        pltpu.make_async_copy(src, dst, load_sem.at[i])
        for i, (src, dst) in enumerate(
            [
                (obj_hbm, obj),
                (pos_hbm, pos_ref),
                (probe_hbm, probe),
                (table_hbm, table),
                (amp_hbm, amp),
                (proj_hbm, proj),
            ]
        )
    ]
    for load in loads[:5]:
        load.start()
    barrier = pltpu.get_barrier_semaphore()
    greeted = [x_peer(d) for d in x_steps] + [y_peer(d) for d in y_steps]
    greeted += [z_peer(d) for d in z_steps] + [sibling]
    for device in greeted:
        pl.semaphore_signal(barrier, inc=1, device_id=device, device_id_type=MESH)
    loads[0].wait()
    for part in range(2):
        bands[part, t, c] = obj[part].astype(BF16)
    pl.semaphore_wait(barrier, len(greeted))

    first, second = {}, {}

    def go_x(part, tt, cc, key):
        for d in x_steps:
            block = bands.at[part, tt, cc]
            key[d] = remote(block, block, x_peer(d))

    def go_y(part, tt, cc, key):
        for d in y_steps:
            block = bands.at[part, tt, cc]
            key[d] = remote(block, block, y_peer(d))

    for part in range(2):
        first[part] = {}
        second[part, 0] = {}
    go_x(0, t, c, first[0])
    go_y(1, t, c, first[1])
    go_y(0, t, c, second[0, 0])
    go_x(1, t, c, second[1, 0])
    loads[5].start()

    terms_zero = jnp.zeros((pad, LANES), F32)

    @pl.loop(0, n_patch)
    def _(p):
        for part in range(2):
            terms[p, part, :pad] = terms_zero
            terms[p, part, pad + width :] = terms_zero

    loads[2].wait()
    loads[3].wait()
    f_re, f_im = table[:, :width], table[:, width:]
    fwd[...] = quad(f_re, f_im, -f_im, f_re)
    bwd[...] = quad(f_re, -f_im, f_im, f_re)

    def unpack(part, tt, cc):
        at = pl.ds(pl.multiple_of((tt * n_cuts + cc) * rows, rows), rows)
        block = bands[part, tt, cc]
        for j in range(strips):
            image[part, j, at, :] = block[:, j * LANES : (j + 1) * LANES].astype(F32)

    unpack(0, t, c)
    unpack(1, t, c)
    for i in range(max(len(x_steps), len(y_steps))):
        if i < len(x_steps):
            d = x_steps[i]
            first[0][d].wait_recv()
            second[0, d] = {}
            go_y(0, behind(t, d, n_tile), c, second[0, d])
        if i < len(y_steps):
            d = y_steps[i]
            first[1][d].wait_recv()
            second[1, d] = {}
            go_x(1, t, behind(c, d, n_cuts), second[1, d])
    for d in x_steps:
        unpack(0, behind(t, d, n_tile), c)
    for d in y_steps:
        unpack(1, t, behind(c, d, n_cuts))
    for d in [0] + x_steps:
        for e in y_steps:
            second[0, d][e].wait_recv()
            unpack(0, behind(t, d, n_tile), behind(c, e, n_cuts))
    for d in [0] + y_steps:
        for e in x_steps:
            second[1, d][e].wait_recv()
            unpack(1, behind(t, e, n_tile), behind(c, d, n_cuts))
    loads[4].wait()
    loads[1].wait()

    lane = lax.broadcasted_iota(jnp.int32, (width, LANES), 1)

    def pair(i, carry):
        exits = []
        p_re, p_im = probe[0], probe[1]
        for k in range(2):
            row, col = pos_ref[0, 2 * i + k], pos_ref[1, 2 * i + k]
            strip, shift = col // LANES, lax.rem(col, LANES)

            def window(part):
                left = image[part, strip, pl.ds(row, width), :]
                right = image[part, jnp.minimum(strip + 1, strips - 1), pl.ds(row, width), :]
                joined = jnp.where(lane >= shift, left, right)
                return pltpu.roll(joined, lax.rem(LANES - shift, LANES), 1)

            w_re, w_im = window(0), window(1)
            exits.append((p_re * w_re - p_im * w_im, p_re * w_im + p_im * w_re))
        spread = dot(quad(*exits[0], *exits[1]).astype(BF16), fwd[...]).astype(BF16)
        spectrum = dot(bwd[...], swap(spread))
        s_re, s_im = spectrum[:width], spectrum[width:]
        measured = jnp.concatenate([amp[2 * i], amp[2 * i + 1]], axis=1).astype(F32)
        scaling = measured * lax.rsqrt(jnp.maximum(s_re * s_re + s_im * s_im, 1.0))
        projected = jnp.concatenate([s_re * scaling, s_im * scaling], axis=0).astype(BF16)
        back = dot(swap(projected), bwd[...]).astype(BF16)
        revised = dot(fwd[...], swap(back))
        for k in range(2):
            shift = lax.rem(pos_ref[1, 2 * i + k], LANES)
            cols = slice(k * width, (k + 1) * width)
            d_re = revised[:width, cols] - exits[k][0]
            d_im = revised[width:, cols] - exits[k][1]
            u_re = STEP_SIZE * (p_re * d_re + p_im * d_im)
            u_im = STEP_SIZE * (p_re * d_im - p_im * d_re)
            terms[2 * i + k, 0, pad : pad + width] = pltpu.roll(u_re, shift, 1)
            terms[2 * i + k, 1, pad : pad + width] = pltpu.roll(u_im, shift, 1)
        return carry

    lax.fori_loop(0, n_patch // 2, pair, 0, unroll=True)

    piece = 64
    lane8 = lax.broadcasted_iota(jnp.int32, (8, LANES), 1)

    def build(part, slab):
        for q in range(n_cuts * rows // piece):
            base = pad + slab * (n_cuts * rows) + q * piece

            def add(p, totals):
                row, col = pos_ref[0, p], pos_ref[1, p]
                strip, shift = col // LANES, lax.rem(col, LANES)
                block = terms[p, part, pl.ds(base - row, piece), :].reshape(piece // 8, 8, LANES)
                place = strip + jnp.where(lane8 < shift, 1, 0)
                return tuple(
                    total + jnp.where((place == j)[None], block, 0.0)
                    for j, total in enumerate(totals)
                )

            zero = jnp.zeros((piece // 8, 8, LANES), F32)
            totals = lax.fori_loop(0, n_patch, add, (zero,) * strips, unroll=True)
            for h in range(2):
                wide = jnp.concatenate(
                    [x.reshape(piece, LANES) for x in totals[h * strips // 2 : (h + 1) * strips // 2]],
                    axis=1,
                ).astype(BF16)
                for b in range(piece // rows):
                    canvas[part, h, slab, q * (piece // rows) + b] = wide[b * rows : (b + 1) * rows]

    sum_x, sum_y = {}, {}
    for d in reversed(x_steps):
        slab = ahead(t, d, n_tile)
        build(1, slab)
        sum_x[d] = remote(canvas.at[1, 0, slab], first_x.at[d - 1], x_peer(d))
    build(1, t)
    for d in reversed(y_steps):
        sum_y[d] = remote(canvas.at[1, 1, :, ahead(c, d, n_cuts)], first_y.at[d - 1], y_peer(d))
    for d in reversed(x_steps):
        build(0, ahead(t, d, n_tile))
    build(0, t)

    fin_x, fin_y = {}, {}
    for d in x_steps:
        sum_x[d].wait_recv()
    total = canvas[1, 0, t].astype(F32)
    for d in x_steps:
        total = total + first_x[d - 1].astype(F32)
    slab_sum[0] = total
    staged[0] = total.astype(BF16)
    for d in reversed(y_steps):
        fin_y[d] = remote(staged.at[0, ahead(c, d, n_cuts)], last_y.at[d - 1], y_peer(d))
    for d in y_steps:
        sum_y[d].wait_recv()
    for tt in range(n_tile):
        total = canvas[1, 1, tt, c].astype(F32)
        for d in y_steps:
            total = total + first_y[d - 1, tt].astype(F32)
        slab_sum[1, tt] = total
        staged[1, tt] = total.astype(BF16)
    for d in reversed(x_steps):
        fin_x[d] = remote(staged.at[1, ahead(t, d, n_tile)], last_x.at[d - 1], x_peer(d))
    for d in y_steps:
        fin_y[d].wait_recv()
    left = slab_sum[0, c]
    for d in y_steps:
        left = left + last_y[d - 1].astype(F32)
    for d in x_steps:
        fin_x[d].wait_recv()
    right = slab_sum[1, t]
    for d in x_steps:
        right = right + last_x[d - 1].astype(F32)
    update = jnp.concatenate([left, right], axis=1)
    phase[a, c] = (bands[1, t, c].astype(F32) + update).astype(BF16)
    new_ref[1] = obj[1] + update

    z_copies, y_copies, far_copies, s_copies = {}, {}, {}, {}
    order = [0] + z_steps
    opposite = n_cuts // 2
    near = [1, n_cuts - 1]
    close = z_steps[:4]

    def angle_of(dz, which):
        return behind(z, dz, n_z) * CORES + which

    def block_at(dz, dc):
        return phase.at[angle_of(dz, core), behind(c, dc, n_cuts)]

    own = block_at(0, 0)
    y_copies[0, opposite] = remote(own, own, y_peer(opposite))
    for dz in z_steps:
        z_copies[dz] = remote(own, own, z_peer(dz))

    real_x, real_y = {}, {}

    def real_begin():
        for d in reversed(x_steps):
            real_x[d] = remote(
                canvas.at[0, :, ahead(t, d, n_tile)], real_first.at[d - 1], x_peer(d)
            )

    def real_middle():
        for d in x_steps:
            real_x[d].wait_recv()
        for h in range(2):
            total = canvas[0, h, t].astype(F32)
            for d in x_steps:
                total = total + real_first[d - 1, h].astype(F32)
            real_sum[h] = total
            for cc in range(n_cuts):
                real_staged[cc, h] = total[cc].astype(BF16)
        for d in y_steps:
            real_y[d] = remote(real_staged.at[ahead(c, d, n_cuts)], real_last.at[d - 1], y_peer(d))

    def real_end():
        for d in y_steps:
            real_y[d].wait_recv()
        for h in range(2):
            total = real_sum[h, c]
            for d in y_steps:
                total = total + real_last[d - 1, h].astype(F32)
            cols = slice(h * half, (h + 1) * half)
            new_ref[0, :, cols] = obj[0, :, cols] + total

    def project(angle, start):
        block = phase[angle].reshape(n_cuts * rows, pixels)
        weights = proj[pl.ds(pl.multiple_of(angle * pixels, pixels), pixels), :]
        term = dot(block, weights)
        if start:
            vol_ref[...] = term
        else:
            vol_ref[...] += term

    def to_sibling(dz, dc):
        block = block_at(dz, dc)
        s_copies[dz, dc] = remote(block, block, sibling)

    for dc in near:
        y_copies[0, dc] = remote(own, own, y_peer(dc))
    to_sibling(0, 0)
    real_begin()
    y_copies[0, opposite].wait_recv()
    to_sibling(0, opposite)
    block = block_at(0, opposite)
    for dz in close:
        far_copies[dz] = remote(block, block, z_peer(dz))
    for dz in z_steps:
        z_copies[dz].wait_recv()
        block = block_at(dz, 0)
        for dc in near if dz in close else [opposite] + near:
            y_copies[dz, dc] = remote(block, block, y_peer(dc))
        to_sibling(dz, 0)
    real_middle()
    loads[5].wait()
    for dz in order:
        for dc in near + [opposite]:
            if dc == opposite and dz in close:
                far_copies[dz].wait_recv()
            elif (dz, dc) != (0, opposite):
                y_copies[dz, dc].wait_recv()
            if (dz, dc) != (0, opposite):
                to_sibling(dz, dc)
        project(angle_of(dz, core), dz == 0)
    real_end()
    for dz in order:
        for dc in range(n_cuts):
            s_copies[dz, dc].wait_recv()
        project(angle_of(dz, 1 - core), False)
    for copy in sent:
        copy.wait_send()


def hand_on(new_src, vol_src, new_ref, vol_ref, new_held, vol_held, sem):
    way_in = [
        pltpu.make_async_copy(new_src, new_held, sem.at[0]),
        pltpu.make_async_copy(vol_src, vol_held, sem.at[1]),
    ]
    way_out = [
        pltpu.make_async_copy(new_held, new_ref, sem.at[2]),
        pltpu.make_async_copy(vol_held, vol_ref, sem.at[3]),
    ]
    for copy in way_in:
        copy.start()
    for copy, onward in zip(way_in, way_out):
        copy.wait()
        onward.start()
    for copy in way_out:
        copy.wait()


def body(objects, illumination, positions, amplitudes, projector):
    n_angle, n_tile, n_cuts = (lax.axis_size(n) for n in ("angle", "tile", "cuts"))
    _, _, rows, pixels = objects.shape
    n_patch = positions.shape[1]
    width = illumination.shape[-1]
    strips = pixels // LANES
    half = pixels // 2
    pad = pixels - width
    vmem = pl.BlockSpec(memory_space=pltpu.VMEM)
    hbm = pl.BlockSpec(memory_space=pltpu.HBM)

    new_objects, volume = pl.pallas_call(
        functools.partial(kernel, n_angle, n_tile, n_cuts),
        out_shape=(
            jax.ShapeDtypeStruct((2, rows, pixels), F32),
            jax.ShapeDtypeStruct((n_cuts * rows, projector.shape[1]), F32),
        ),
        in_specs=[hbm] * 6,
        out_specs=(vmem, vmem),
        scratch_shapes=[
            pltpu.VMEM((2, rows, pixels), F32),
            pltpu.VMEM((n_patch, width, width), BF16),
            pltpu.VMEM((2, width, width), F32),
            pltpu.VMEM((width, 2 * width), BF16),
            pltpu.VMEM(projector.shape, BF16),
            pltpu.VMEM((2, n_tile, n_cuts, rows, pixels), BF16),
            pltpu.VMEM((2, strips, pixels, LANES), F32),
            pltpu.VMEM((2 * width, 2 * width), BF16),
            pltpu.VMEM((2 * width, 2 * width), BF16),
            pltpu.VMEM((n_patch, 2, 2 * pad + width, LANES), F32),
            pltpu.VMEM((2, 2, n_tile, n_cuts, rows, half), BF16),
            pltpu.VMEM((n_tile - 1, n_cuts, rows, half), BF16),
            pltpu.VMEM((n_cuts - 1, n_tile, rows, half), BF16),
            pltpu.VMEM((2, n_cuts, rows, half), F32),
            pltpu.VMEM((2, n_cuts, rows, half), BF16),
            pltpu.VMEM((n_tile - 1, rows, half), BF16),
            pltpu.VMEM((n_cuts - 1, rows, half), BF16),
            pltpu.VMEM((n_tile - 1, 2, n_cuts, rows, half), BF16),
            pltpu.VMEM((2, n_cuts, rows, half), F32),
            pltpu.VMEM((n_cuts, 2, rows, half), BF16),
            pltpu.VMEM((n_cuts - 1, 2, rows, half), BF16),
            pltpu.VMEM((n_angle, n_cuts, rows, pixels), BF16),
            pltpu.SMEM((2, n_patch), jnp.int32),
            pltpu.SemaphoreType.DMA((6,)),
            pltpu.SemaphoreType.DMA((COPIES,)),
            pltpu.SemaphoreType.DMA((COPIES,)),
        ],
        compiler_params=pltpu.CompilerParams(
            collective_id=0, has_side_effects=True, vmem_limit_bytes=56 * 2**20
        ),
        name="update_and_project",
    )(positions[0].T, objects[0], amplitudes[0], illumination, dft_table(width), projector)
    any_place = pl.BlockSpec(memory_space=pl.ANY)
    new_objects, volume = pl.pallas_call(
        hand_on,
        out_shape=(
            jax.ShapeDtypeStruct(new_objects.shape, F32),
            jax.ShapeDtypeStruct(volume.shape, F32),
        ),
        in_specs=[any_place] * 2,
        out_specs=(any_place, any_place),
        scratch_shapes=[
            pltpu.VMEM(new_objects.shape, F32),
            pltpu.VMEM(volume.shape, F32),
            pltpu.SemaphoreType.DMA((4,)),
        ],
        name="hand_on",
    )(new_objects, volume)
    return new_objects[None], volume


def solution(mesh):
    in_specs = (
        P("angle", None, ("tile", "cuts"), None),
        P(),
        P("angle", ("tile", "cuts"), None),
        P("angle", ("tile", "cuts"), None, None),
        P(None, ("angle", "cuts")),
    )
    out_specs = (P("angle", None, ("tile", "cuts"), None), P("tile", ("angle", "cuts")))
    return jax.shard_map(body, mesh=mesh, in_specs=in_specs, out_specs=out_specs, check_vma=False)
```

```python
import functools

import jax
import jax.numpy as jnp
import numpy as np
from jax import lax
from jax.experimental import pallas as pl
from jax.experimental.pallas import tpu as pltpu
from jax.sharding import PartitionSpec as P

MESH = pl.DeviceIdType.MESH
STEP_SIZE = 0.1
LANES = 128
CORES = 2
COPIES = 160
F32, BF16 = jnp.float32, jnp.bfloat16


def dft_table(width):
    index = np.arange(width)
    phase = (index[:, None] * index[None, :] % width) * (2.0 * np.pi / width)
    scale = 1.0 / np.sqrt(width)
    table = np.concatenate([np.cos(phase) * scale, -np.sin(phase) * scale], axis=1)
    return jnp.asarray(table.astype(np.float32)).astype(BF16)


def dot(a, b):
    return jnp.dot(a, b, preferred_element_type=F32)


def quad(a, b, c, d):
    return jnp.concatenate(
        [jnp.concatenate([a, b], axis=1), jnp.concatenate([c, d], axis=1)], axis=0
    )


def swap(x):
    w = x.shape[0] // 2
    return quad(x[:w, :w], x[w:, :w], x[:w, w:], x[w:, w:])


def near_first(n):
    return sorted(range(1, n), key=lambda d: min(d, n - d))


def kernel(
    n_angle,
    n_tile,
    n_cuts,
    pos_hbm,
    obj_hbm,
    amp_hbm,
    probe_hbm,
    table_hbm,
    proj_hbm,
    new_ref,
    vol_ref,
    obj,
    amp,
    probe,
    table,
    proj,
    bands,
    image,
    fwd,
    bwd,
    terms,
    canvas,
    first_x,
    first_y,
    slab_sum,
    staged,
    last_x,
    last_y,
    real_first,
    real_sum,
    real_staged,
    real_last,
    phase,
    pos_ref,
    load_sem,
    send_sem,
    recv_sem,
):
    a, t, c = lax.axis_index("angle"), lax.axis_index("tile"), lax.axis_index("cuts")
    z, core = a // CORES, lax.rem(a, CORES)
    n_z = n_angle // CORES
    rows, pixels = obj.shape[1:]
    width = probe.shape[-1]
    strips = pixels // LANES
    half = pixels // 2
    n_patch = amp.shape[0]
    pad = pixels - width
    x_steps, y_steps, z_steps = near_first(n_tile), near_first(n_cuts), near_first(n_z)

    def ahead(at, step, n):
        return lax.rem(at + step, n)

    def behind(at, step, n):
        return lax.rem(at + n - step, n)

    def x_peer(d):
        return {"tile": ahead(t, d, n_tile)}

    def y_peer(d):
        return {"cuts": ahead(c, d, n_cuts)}

    def z_peer(d):
        return {"angle": ahead(z, d, n_z) * CORES + core}

    sibling = {"angle": z * CORES + (1 - core)}
    sent = []

    def remote(src, dst, device):
        i = len(sent)
        copy = pltpu.make_async_remote_copy(
            src_ref=src,
            dst_ref=dst,
            send_sem=send_sem.at[i],
            recv_sem=recv_sem.at[i],
            device_id=device,
            device_id_type=MESH,
        )
        copy.start()
        sent.append(copy)
        return copy

    loads = [
        pltpu.make_async_copy(src, dst, load_sem.at[i])
        for i, (src, dst) in enumerate(
            [
                (obj_hbm, obj),
                (pos_hbm, pos_ref),
                (probe_hbm, probe),
                (table_hbm, table),
                (amp_hbm, amp),
                (proj_hbm, proj),
            ]
        )
    ]
    for load in loads[:5]:
        load.start()
    barrier = pltpu.get_barrier_semaphore()
    greeted = [x_peer(d) for d in x_steps] + [y_peer(d) for d in y_steps]
    greeted += [z_peer(d) for d in z_steps] + [sibling]
    for device in greeted:
        pl.semaphore_signal(barrier, inc=1, device_id=device, device_id_type=MESH)
    loads[0].wait()
    for part in range(2):
        bands[part, t, c] = obj[part].astype(BF16)
    pl.semaphore_wait(barrier, len(greeted))

    first, second = {}, {}

    def go_x(part, tt, cc, key):
        for d in x_steps:
            block = bands.at[part, tt, cc]
            key[d] = remote(block, block, x_peer(d))

    def go_y(part, tt, cc, key):
        for d in y_steps:
            block = bands.at[part, tt, cc]
            key[d] = remote(block, block, y_peer(d))

    for part in range(2):
        first[part] = {}
        second[part, 0] = {}
    go_x(0, t, c, first[0])
    go_y(1, t, c, first[1])
    go_y(0, t, c, second[0, 0])
    go_x(1, t, c, second[1, 0])
    loads[5].start()

    terms_zero = jnp.zeros((pad, LANES), F32)

    @pl.loop(0, n_patch)
    def _(p):
        for part in range(2):
            terms[p, part, :pad] = terms_zero
            terms[p, part, pad + width :] = terms_zero

    loads[2].wait()
    loads[3].wait()
    f_re, f_im = table[:, :width], table[:, width:]
    fwd[...] = quad(f_re, f_im, -f_im, f_re)
    bwd[...] = quad(f_re, -f_im, f_im, f_re)

    def unpack(part, tt, cc):
        at = pl.ds(pl.multiple_of((tt * n_cuts + cc) * rows, rows), rows)
        block = bands[part, tt, cc]
        for j in range(strips):
            image[part, j, at, :] = block[:, j * LANES : (j + 1) * LANES].astype(F32)

    unpack(0, t, c)
    unpack(1, t, c)
    for i in range(max(len(x_steps), len(y_steps))):
        if i < len(x_steps):
            d = x_steps[i]
            first[0][d].wait_recv()
            second[0, d] = {}
            go_y(0, behind(t, d, n_tile), c, second[0, d])
        if i < len(y_steps):
            d = y_steps[i]
            first[1][d].wait_recv()
            second[1, d] = {}
            go_x(1, t, behind(c, d, n_cuts), second[1, d])
    for d in x_steps:
        unpack(0, behind(t, d, n_tile), c)
    for d in y_steps:
        unpack(1, t, behind(c, d, n_cuts))
    for d in [0] + x_steps:
        for e in y_steps:
            second[0, d][e].wait_recv()
            unpack(0, behind(t, d, n_tile), behind(c, e, n_cuts))
    for d in [0] + y_steps:
        for e in x_steps:
            second[1, d][e].wait_recv()
            unpack(1, behind(t, e, n_tile), behind(c, d, n_cuts))
    loads[4].wait()
    loads[1].wait()

    lane = lax.broadcasted_iota(jnp.int32, (width, LANES), 1)

    def pair(i, carry):
        exits = []
        p_re, p_im = probe[0], probe[1]
        for k in range(2):
            row, col = pos_ref[0, 2 * i + k], pos_ref[1, 2 * i + k]
            strip, shift = col // LANES, lax.rem(col, LANES)

            def window(part):
                left = image[part, strip, pl.ds(row, width), :]
                right = image[part, jnp.minimum(strip + 1, strips - 1), pl.ds(row, width), :]
                joined = jnp.where(lane >= shift, left, right)
                return pltpu.roll(joined, lax.rem(LANES - shift, LANES), 1)

            w_re, w_im = window(0), window(1)
            exits.append((p_re * w_re - p_im * w_im, p_re * w_im + p_im * w_re))
        spread = dot(quad(*exits[0], *exits[1]).astype(BF16), fwd[...]).astype(BF16)
        spectrum = dot(bwd[...], swap(spread))
        s_re, s_im = spectrum[:width], spectrum[width:]
        measured = jnp.concatenate([amp[2 * i], amp[2 * i + 1]], axis=1).astype(F32)
        scaling = measured * lax.rsqrt(jnp.maximum(s_re * s_re + s_im * s_im, 1.0))
        projected = jnp.concatenate([s_re * scaling, s_im * scaling], axis=0).astype(BF16)
        back = dot(swap(projected), bwd[...]).astype(BF16)
        revised = dot(fwd[...], swap(back))
        for k in range(2):
            shift = lax.rem(pos_ref[1, 2 * i + k], LANES)
            cols = slice(k * width, (k + 1) * width)
            d_re = revised[:width, cols] - exits[k][0]
            d_im = revised[width:, cols] - exits[k][1]
            u_re = STEP_SIZE * (p_re * d_re + p_im * d_im)
            u_im = STEP_SIZE * (p_re * d_im - p_im * d_re)
            terms[2 * i + k, 0, pad : pad + width] = pltpu.roll(u_re, shift, 1)
            terms[2 * i + k, 1, pad : pad + width] = pltpu.roll(u_im, shift, 1)
        return carry

    lax.fori_loop(0, n_patch // 2, pair, 0, unroll=True)

    piece = 64
    lane8 = lax.broadcasted_iota(jnp.int32, (8, LANES), 1)

    def build(part, slab):
        for q in range(n_cuts * rows // piece):
            base = pad + slab * (n_cuts * rows) + q * piece

            def add(p, totals):
                row, col = pos_ref[0, p], pos_ref[1, p]
                strip, shift = col // LANES, lax.rem(col, LANES)
                block = terms[p, part, pl.ds(base - row, piece), :].reshape(piece // 8, 8, LANES)
                place = strip + jnp.where(lane8 < shift, 1, 0)
                return tuple(
                    total + jnp.where((place == j)[None], block, 0.0)
                    for j, total in enumerate(totals)
                )

            zero = jnp.zeros((piece // 8, 8, LANES), F32)
            totals = lax.fori_loop(0, n_patch, add, (zero,) * strips, unroll=True)
            for h in range(2):
                wide = jnp.concatenate(
                    [x.reshape(piece, LANES) for x in totals[h * strips // 2 : (h + 1) * strips // 2]],
                    axis=1,
                ).astype(BF16)
                for b in range(piece // rows):
                    canvas[part, h, slab, q * (piece // rows) + b] = wide[b * rows : (b + 1) * rows]

    sum_x, sum_y = {}, {}
    for d in reversed(x_steps):
        slab = ahead(t, d, n_tile)
        build(1, slab)
        sum_x[d] = remote(canvas.at[1, 0, slab], first_x.at[d - 1], x_peer(d))
    build(1, t)
    for d in reversed(y_steps):
        sum_y[d] = remote(canvas.at[1, 1, :, ahead(c, d, n_cuts)], first_y.at[d - 1], y_peer(d))
    for d in reversed(x_steps):
        build(0, ahead(t, d, n_tile))
    build(0, t)

    fin_x, fin_y = {}, {}
    for d in x_steps:
        sum_x[d].wait_recv()
    total = canvas[1, 0, t].astype(F32)
    for d in x_steps:
        total = total + first_x[d - 1].astype(F32)
    slab_sum[0] = total
    staged[0] = total.astype(BF16)
    for d in reversed(y_steps):
        fin_y[d] = remote(staged.at[0, ahead(c, d, n_cuts)], last_y.at[d - 1], y_peer(d))
    for d in y_steps:
        sum_y[d].wait_recv()
    for tt in range(n_tile):
        total = canvas[1, 1, tt, c].astype(F32)
        for d in y_steps:
            total = total + first_y[d - 1, tt].astype(F32)
        slab_sum[1, tt] = total
        staged[1, tt] = total.astype(BF16)
    for d in reversed(x_steps):
        fin_x[d] = remote(staged.at[1, ahead(t, d, n_tile)], last_x.at[d - 1], x_peer(d))
    for d in y_steps:
        fin_y[d].wait_recv()
    left = slab_sum[0, c]
    for d in y_steps:
        left = left + last_y[d - 1].astype(F32)
    for d in x_steps:
        fin_x[d].wait_recv()
    right = slab_sum[1, t]
    for d in x_steps:
        right = right + last_x[d - 1].astype(F32)
    update = jnp.concatenate([left, right], axis=1)
    phase[a, c] = (bands[1, t, c].astype(F32) + update).astype(BF16)
    new_ref[1] = obj[1] + update

    z_copies, y_copies, far_copies, s_copies = {}, {}, {}, {}
    order = [0] + z_steps
    opposite = n_cuts // 2
    near = [1, n_cuts - 1]
    close = z_steps[:4]

    def angle_of(dz, which):
        return behind(z, dz, n_z) * CORES + which

    def block_at(dz, dc):
        return phase.at[angle_of(dz, core), behind(c, dc, n_cuts)]

    own = block_at(0, 0)
    y_copies[0, opposite] = remote(own, own, y_peer(opposite))
    for dz in z_steps:
        z_copies[dz] = remote(own, own, z_peer(dz))

    real_x, real_y = {}, {}

    def real_begin():
        for d in reversed(x_steps):
            real_x[d] = remote(
                canvas.at[0, :, ahead(t, d, n_tile)], real_first.at[d - 1], x_peer(d)
            )

    def real_middle():
        for d in x_steps:
            real_x[d].wait_recv()
        for h in range(2):
            total = canvas[0, h, t].astype(F32)
            for d in x_steps:
                total = total + real_first[d - 1, h].astype(F32)
            real_sum[h] = total
            for cc in range(n_cuts):
                real_staged[cc, h] = total[cc].astype(BF16)
        for d in y_steps:
            real_y[d] = remote(real_staged.at[ahead(c, d, n_cuts)], real_last.at[d - 1], y_peer(d))

    def real_end():
        for d in y_steps:
            real_y[d].wait_recv()
        for h in range(2):
            total = real_sum[h, c]
            for d in y_steps:
                total = total + real_last[d - 1, h].astype(F32)
            cols = slice(h * half, (h + 1) * half)
            new_ref[0, :, cols] = obj[0, :, cols] + total

    def project(angle, start):
        block = phase[angle].reshape(n_cuts * rows, pixels)
        weights = proj[pl.ds(pl.multiple_of(angle * pixels, pixels), pixels), :]
        term = dot(block, weights)
        if start:
            vol_ref[...] = term
        else:
            vol_ref[...] += term

    def to_sibling(dz, dc):
        block = block_at(dz, dc)
        s_copies[dz, dc] = remote(block, block, sibling)

    for dc in near:
        y_copies[0, dc] = remote(own, own, y_peer(dc))
    to_sibling(0, 0)
    real_begin()
    y_copies[0, opposite].wait_recv()
    to_sibling(0, opposite)
    block = block_at(0, opposite)
    for dz in close:
        far_copies[dz] = remote(block, block, z_peer(dz))
    for dz in z_steps:
        z_copies[dz].wait_recv()
        block = block_at(dz, 0)
        for dc in near if dz in close else [opposite] + near:
            y_copies[dz, dc] = remote(block, block, y_peer(dc))
        to_sibling(dz, 0)
    real_middle()
    loads[5].wait()
    for dz in order:
        for dc in near + [opposite]:
            if dc == opposite and dz in close:
                far_copies[dz].wait_recv()
            elif (dz, dc) != (0, opposite):
                y_copies[dz, dc].wait_recv()
            if (dz, dc) != (0, opposite):
                to_sibling(dz, dc)
        project(angle_of(dz, core), dz == 0)
    real_end()
    for dz in order:
        for dc in range(n_cuts):
            s_copies[dz, dc].wait_recv()
        project(angle_of(dz, 1 - core), False)
    for copy in sent:
        copy.wait_send()


def hand_on(new_src, vol_src, new_ref, vol_ref, sem):
    copies = [
        pltpu.make_async_copy(new_src, new_ref, sem.at[0]),
        pltpu.make_async_copy(vol_src, vol_ref, sem.at[1]),
    ]
    for copy in copies:
        copy.start()
    for copy in copies:
        copy.wait()


def body(objects, illumination, positions, amplitudes, projector):
    n_angle, n_tile, n_cuts = (lax.axis_size(n) for n in ("angle", "tile", "cuts"))
    _, _, rows, pixels = objects.shape
    n_patch = positions.shape[1]
    width = illumination.shape[-1]
    strips = pixels // LANES
    half = pixels // 2
    pad = pixels - width
    vmem = pl.BlockSpec(memory_space=pltpu.VMEM)
    hbm = pl.BlockSpec(memory_space=pltpu.HBM)

    operands = (
        positions[0].T, objects[0], amplitudes[0], illumination, dft_table(width), projector
    )
    new_objects, volume = pl.pallas_call(
        functools.partial(kernel, n_angle, n_tile, n_cuts),
        out_shape=(
            pltpu.VMEM((2, rows, pixels), F32),
            pltpu.VMEM((n_cuts * rows, projector.shape[1]), F32),
        ),
        in_specs=[hbm] * 6,
        out_specs=(vmem, vmem),
        scratch_shapes=[
            pltpu.VMEM((2, rows, pixels), F32),
            pltpu.VMEM((n_patch, width, width), BF16),
            pltpu.VMEM((2, width, width), F32),
            pltpu.VMEM((width, 2 * width), BF16),
            pltpu.VMEM(projector.shape, BF16),
            pltpu.VMEM((2, n_tile, n_cuts, rows, pixels), BF16),
            pltpu.VMEM((2, strips, pixels, LANES), F32),
            pltpu.VMEM((2 * width, 2 * width), BF16),
            pltpu.VMEM((2 * width, 2 * width), BF16),
            pltpu.VMEM((n_patch, 2, 2 * pad + width, LANES), F32),
            pltpu.VMEM((2, 2, n_tile, n_cuts, rows, half), BF16),
            pltpu.VMEM((n_tile - 1, n_cuts, rows, half), BF16),
            pltpu.VMEM((n_cuts - 1, n_tile, rows, half), BF16),
            pltpu.VMEM((2, n_cuts, rows, half), F32),
            pltpu.VMEM((2, n_cuts, rows, half), BF16),
            pltpu.VMEM((n_tile - 1, rows, half), BF16),
            pltpu.VMEM((n_cuts - 1, rows, half), BF16),
            pltpu.VMEM((n_tile - 1, 2, n_cuts, rows, half), BF16),
            pltpu.VMEM((2, n_cuts, rows, half), F32),
            pltpu.VMEM((n_cuts, 2, rows, half), BF16),
            pltpu.VMEM((n_cuts - 1, 2, rows, half), BF16),
            pltpu.VMEM((n_angle, n_cuts, rows, pixels), BF16),
            pltpu.SMEM((2, n_patch), jnp.int32),
            pltpu.SemaphoreType.DMA((6,)),
            pltpu.SemaphoreType.DMA((COPIES,)),
            pltpu.SemaphoreType.DMA((COPIES,)),
        ],
        compiler_params=pltpu.CompilerParams(
            collective_id=0, has_side_effects=True, vmem_limit_bytes=44 * 2**20
        ),
        name="update_and_project",
    )(*(pltpu.with_memory_space_constraint(x, pltpu.HBM) for x in operands))
    any_place = pl.BlockSpec(memory_space=pl.ANY)
    new_objects, volume = pl.pallas_call(
        hand_on,
        out_shape=(
            jax.ShapeDtypeStruct(new_objects.shape, F32),
            jax.ShapeDtypeStruct(volume.shape, F32),
        ),
        in_specs=[vmem] * 2,
        out_specs=(any_place, any_place),
        scratch_shapes=[
            pltpu.SemaphoreType.DMA((2,)),
        ],
        name="hand_on",
    )(*(pltpu.with_memory_space_constraint(x, pltpu.VMEM) for x in (new_objects, volume)))
    return new_objects[None], volume


def solution(mesh):
    in_specs = (
        P("angle", None, ("tile", "cuts"), None),
        P(),
        P("angle", ("tile", "cuts"), None),
        P("angle", ("tile", "cuts"), None, None),
        P(None, ("angle", "cuts")),
    )
    out_specs = (P("angle", None, ("tile", "cuts"), None), P("tile", ("angle", "cuts")))
    return jax.shard_map(body, mesh=mesh, in_specs=in_specs, out_specs=out_specs, check_vma=False)
```

```python
import functools

import jax
import jax.numpy as jnp
import numpy as np
from jax import lax
from jax.experimental import pallas as pl
from jax.experimental.pallas import tpu as pltpu
from jax.sharding import PartitionSpec as P

MESH = pl.DeviceIdType.MESH
STEP_SIZE = 0.1
LANES = 128
CORES = 2
COPIES = 160
F32, BF16 = jnp.float32, jnp.bfloat16


def dft_table(width):
    index = np.arange(width)
    phase = (index[:, None] * index[None, :] % width) * (2.0 * np.pi / width)
    scale = 1.0 / np.sqrt(width)
    table = np.concatenate([np.cos(phase) * scale, -np.sin(phase) * scale], axis=1)
    return jnp.asarray(table.astype(np.float32)).astype(BF16)


def dot(a, b):
    return jnp.dot(a, b, preferred_element_type=F32)


def quad(a, b, c, d):
    return jnp.concatenate(
        [jnp.concatenate([a, b], axis=1), jnp.concatenate([c, d], axis=1)], axis=0
    )


def swap(x):
    w = x.shape[0] // 2
    return quad(x[:w, :w], x[w:, :w], x[:w, w:], x[w:, w:])


def near_first(n):
    return sorted(range(1, n), key=lambda d: min(d, n - d))


def kernel(
    n_angle,
    n_tile,
    n_cuts,
    pos_hbm,
    obj_hbm,
    amp_hbm,
    probe_hbm,
    table_hbm,
    proj_hbm,
    new_ref,
    vol_ref,
    obj,
    amp,
    probe,
    table,
    proj,
    bands,
    image,
    fwd,
    bwd,
    terms,
    canvas,
    first_x,
    first_y,
    slab_sum,
    staged,
    last_x,
    last_y,
    real_first,
    real_sum,
    real_staged,
    real_last,
    phase,
    pos_ref,
    load_sem,
    send_sem,
    recv_sem,
):
    a, t, c = lax.axis_index("angle"), lax.axis_index("tile"), lax.axis_index("cuts")
    z, core = a // CORES, lax.rem(a, CORES)
    n_z = n_angle // CORES
    rows, pixels = obj.shape[1:]
    width = probe.shape[-1]
    strips = pixels // LANES
    half = pixels // 2
    n_patch = amp.shape[0]
    pad = pixels - width
    x_steps, y_steps, z_steps = near_first(n_tile), near_first(n_cuts), near_first(n_z)

    def ahead(at, step, n):
        return lax.rem(at + step, n)

    def behind(at, step, n):
        return lax.rem(at + n - step, n)

    def x_peer(d):
        return {"tile": ahead(t, d, n_tile)}

    def y_peer(d):
        return {"cuts": ahead(c, d, n_cuts)}

    def z_peer(d):
        return {"angle": ahead(z, d, n_z) * CORES + core}

    sibling = {"angle": z * CORES + (1 - core)}
    sent = []

    def remote(src, dst, device):
        i = len(sent)
        copy = pltpu.make_async_remote_copy(
            src_ref=src,
            dst_ref=dst,
            send_sem=send_sem.at[i],
            recv_sem=recv_sem.at[i],
            device_id=device,
            device_id_type=MESH,
        )
        copy.start()
        sent.append(copy)
        return copy

    loads = [
        pltpu.make_async_copy(src, dst, load_sem.at[i])
        for i, (src, dst) in enumerate(
            [
                (obj_hbm, obj),
                (pos_hbm, pos_ref),
                (probe_hbm, probe),
                (table_hbm, table),
                (amp_hbm, amp),
                (proj_hbm, proj),
            ]
        )
    ]
    loads[0].start()
    barrier = pltpu.get_barrier_semaphore()
    greeted = [x_peer(d) for d in x_steps] + [y_peer(d) for d in y_steps]
    greeted += [z_peer(d) for d in z_steps] + [sibling]
    for device in greeted:
        pl.semaphore_signal(barrier, inc=1, device_id=device, device_id_type=MESH)
    for load in loads[1:5]:
        load.start()
    loads[0].wait()
    for part in range(2):
        bands[part, t, c] = obj[part].astype(BF16)
    pl.semaphore_wait(barrier, len(greeted))

    first, second = {}, {}

    def go_x(part, tt, cc, key, steps=x_steps):
        for d in steps:
            block = bands.at[part, tt, cc]
            key[d] = remote(block, block, x_peer(d))

    def go_y(part, tt, cc, key, steps=y_steps):
        for d in steps:
            block = bands.at[part, tt, cc]
            key[d] = remote(block, block, y_peer(d))

    for part in range(2):
        first[part] = {}
        second[part, 0] = {}
    go_x(0, t, c, first[0])
    go_y(1, t, c, first[1])
    go_y(0, t, c, second[0, 0])
    go_x(1, t, c, second[1, 0])
    loads[5].start()

    terms_zero = jnp.zeros((pad, LANES), F32)

    @pl.loop(0, n_patch)
    def _(p):
        for part in range(2):
            terms[p, part, :pad] = terms_zero
            terms[p, part, pad + width :] = terms_zero

    loads[2].wait()
    loads[3].wait()
    f_re, f_im = table[:, :width], table[:, width:]
    fwd[...] = quad(f_re, f_im, -f_im, f_re)
    bwd[...] = quad(f_re, -f_im, f_im, f_re)

    def unpack(part, tt, cc):
        at = pl.ds(pl.multiple_of((tt * n_cuts + cc) * rows, rows), rows)
        block = bands[part, tt, cc]
        for j in range(strips):
            image[part, j, at, :] = block[:, j * LANES : (j + 1) * LANES].astype(F32)

    unpack(0, t, c)
    unpack(1, t, c)
    x_far, y_far = n_tile // 2, n_cuts // 2
    x_near, y_near = [d for d in x_steps if d != x_far], [d for d in y_steps if d != y_far]
    turned = {}

    def back_x(d):
        return behind(t, d, n_tile)

    def back_y(d):
        return behind(c, d, n_cuts)

    for dx, dy in zip(x_near, y_near):
        first[0][dx].wait_recv()
        second[0, dx] = {}
        go_y(0, back_x(dx), c, second[0, dx], y_near)
        first[1][dy].wait_recv()
        second[1, dy] = {}
        go_x(1, t, back_y(dy), second[1, dy], x_near)
    first[0][x_far].wait_recv()
    second[0, x_far] = {}
    go_y(0, back_x(x_far), c, second[0, x_far])
    first[1][y_far].wait_recv()
    second[1, y_far] = {}
    go_x(1, t, back_y(y_far), second[1, y_far])
    second[0, 0][y_far].wait_recv()
    turned[0] = {}
    go_x(0, t, back_y(y_far), turned[0], x_near)
    second[1, 0][x_far].wait_recv()
    turned[1] = {}
    go_y(1, back_x(x_far), c, turned[1], y_near)
    for d in x_steps:
        unpack(0, back_x(d), c)
    for d in y_steps:
        unpack(1, t, back_y(d))
    unpack(0, t, back_y(y_far))
    unpack(1, back_x(x_far), c)
    for d in [0] + x_near + [x_far]:
        for e in y_near + [y_far] * (d == x_far):
            second[0, d][e].wait_recv()
            unpack(0, back_x(d), back_y(e))
    for d in [0] + y_near + [y_far]:
        for e in x_near + [x_far] * (d == y_far):
            second[1, d][e].wait_recv()
            unpack(1, back_x(e), back_y(d))
    for d in x_near:
        turned[0][d].wait_recv()
        unpack(0, back_x(d), back_y(y_far))
    for d in y_near:
        turned[1][d].wait_recv()
        unpack(1, back_x(x_far), back_y(d))
    loads[4].wait()
    loads[1].wait()

    lane = lax.broadcasted_iota(jnp.int32, (width, LANES), 1)

    def pair(i, carry):
        exits = []
        p_re, p_im = probe[0], probe[1]
        for k in range(2):
            row, col = pos_ref[0, 2 * i + k], pos_ref[1, 2 * i + k]
            strip, shift = col // LANES, lax.rem(col, LANES)

            def window(part):
                left = image[part, strip, pl.ds(row, width), :]
                right = image[part, jnp.minimum(strip + 1, strips - 1), pl.ds(row, width), :]
                joined = jnp.where(lane >= shift, left, right)
                return pltpu.roll(joined, lax.rem(LANES - shift, LANES), 1)

            w_re, w_im = window(0), window(1)
            exits.append((p_re * w_re - p_im * w_im, p_re * w_im + p_im * w_re))
        spread = dot(quad(*exits[0], *exits[1]).astype(BF16), fwd[...]).astype(BF16)
        spectrum = dot(bwd[...], swap(spread))
        s_re, s_im = spectrum[:width], spectrum[width:]
        measured = jnp.concatenate([amp[2 * i], amp[2 * i + 1]], axis=1).astype(F32)
        scaling = measured * lax.rsqrt(jnp.maximum(s_re * s_re + s_im * s_im, 1.0))
        projected = jnp.concatenate([s_re * scaling, s_im * scaling], axis=0).astype(BF16)
        back = dot(swap(projected), bwd[...]).astype(BF16)
        revised = dot(fwd[...], swap(back))
        for k in range(2):
            shift = lax.rem(pos_ref[1, 2 * i + k], LANES)
            cols = slice(k * width, (k + 1) * width)
            d_re = revised[:width, cols] - exits[k][0]
            d_im = revised[width:, cols] - exits[k][1]
            u_re = STEP_SIZE * (p_re * d_re + p_im * d_im)
            u_im = STEP_SIZE * (p_re * d_im - p_im * d_re)
            terms[2 * i + k, 0, pad : pad + width] = pltpu.roll(u_re, shift, 1)
            terms[2 * i + k, 1, pad : pad + width] = pltpu.roll(u_im, shift, 1)
        return carry

    lax.fori_loop(0, n_patch // 2, pair, 0, unroll=True)

    piece = 64
    lane8 = lax.broadcasted_iota(jnp.int32, (8, LANES), 1)

    pieces = n_cuts * rows // piece

    def build(part, slab, which):
        for q in which:
            base = pad + slab * (n_cuts * rows) + q * piece

            def add(p, totals):
                row, col = pos_ref[0, p], pos_ref[1, p]
                strip, shift = col // LANES, lax.rem(col, LANES)
                block = terms[p, part, pl.ds(base - row, piece), :].reshape(piece // 8, 8, LANES)
                place = strip + jnp.where(lane8 < shift, 1, 0)
                return tuple(
                    total + jnp.where((place == j)[None], block, 0.0)
                    for j, total in enumerate(totals)
                )

            zero = jnp.zeros((piece // 8, 8, LANES), F32)
            totals = lax.fori_loop(0, n_patch, add, (zero,) * strips, unroll=True)
            for h in range(2):
                wide = jnp.concatenate(
                    [x.reshape(piece, LANES) for x in totals[h * strips // 2 : (h + 1) * strips // 2]],
                    axis=1,
                ).astype(BF16)
                for b in range(piece // rows):
                    canvas[part, h, slab, q * (piece // rows) + b] = wide[b * rows : (b + 1) * rows]

    sum_x, sum_y = {}, {}
    pair_size = piece // rows
    mine, odd = c // pair_size, lax.rem(c, pair_size)
    partner = {1: c + 1 - 2 * odd, 2: ahead(c, 2, n_cuts), 3: n_cuts - 1 - c}
    for turn, q in enumerate((1 - mine, mine)):
        part_rows = pl.ds(q * pair_size, pair_size)
        for d in x_steps[::-1] + [0]:
            slab = ahead(t, d, n_tile)
            build(1, slab, [q])
            if d:
                sum_x[d, turn] = remote(
                    canvas.at[1, 0, slab, part_rows], first_x.at[d - 1, part_rows], x_peer(d)
                )
        for m in (2, 3) if turn == 0 else (1,):
            sum_y[m] = remote(
                canvas.at[1, 1, :, partner[m]], first_y.at[m - 1], {"cuts": partner[m]}
            )
    for slab in range(n_tile):
        build(0, slab, range(pieces))

    fin_x, fin_y = {}, {}
    for d in x_steps:
        for turn in range(2):
            sum_x[d, turn].wait_recv()
    total = canvas[1, 0, t].astype(F32)
    for d in x_steps:
        total = total + first_x[d - 1].astype(F32)
    slab_sum[0] = total
    staged[0] = total.astype(BF16)
    for d in reversed(y_steps):
        fin_y[d] = remote(staged.at[0, ahead(c, d, n_cuts)], last_y.at[d - 1], y_peer(d))
    for d in y_steps:
        sum_y[d].wait_recv()
    for tt in range(n_tile):
        total = canvas[1, 1, tt, c].astype(F32)
        for d in y_steps:
            total = total + first_y[d - 1, tt].astype(F32)
        slab_sum[1, tt] = total
        staged[1, tt] = total.astype(BF16)
    for d in reversed(x_steps):
        fin_x[d] = remote(staged.at[1, ahead(t, d, n_tile)], last_x.at[d - 1], x_peer(d))
    for d in y_steps:
        fin_y[d].wait_recv()
    left = slab_sum[0, c]
    for d in y_steps:
        left = left + last_y[d - 1].astype(F32)
    for d in x_steps:
        fin_x[d].wait_recv()
    right = slab_sum[1, t]
    for d in x_steps:
        right = right + last_x[d - 1].astype(F32)
    update = jnp.concatenate([left, right], axis=1)
    phase[a, c] = (bands[1, t, c].astype(F32) + update).astype(BF16)
    new_ref[1] = obj[1] + update

    z_copies, y_copies, far_copies, s_copies = {}, {}, {}, {}
    order = [0] + z_steps
    opposite = n_cuts // 2
    near = [1, n_cuts - 1]
    close = z_steps[:4]

    def angle_of(dz, which):
        return behind(z, dz, n_z) * CORES + which

    def block_at(dz, dc):
        return phase.at[angle_of(dz, core), behind(c, dc, n_cuts)]

    own = block_at(0, 0)
    y_copies[0, opposite] = remote(own, own, y_peer(opposite))
    for dz in z_steps:
        z_copies[dz] = remote(own, own, z_peer(dz))

    real_x, real_y = {}, {}

    def real_begin():
        for d in reversed(x_steps):
            real_x[d] = remote(
                canvas.at[0, :, ahead(t, d, n_tile)], real_first.at[d - 1], x_peer(d)
            )

    def real_middle():
        for d in x_steps:
            real_x[d].wait_recv()
        for h in range(2):
            total = canvas[0, h, t].astype(F32)
            for d in x_steps:
                total = total + real_first[d - 1, h].astype(F32)
            real_sum[h] = total
            for cc in range(n_cuts):
                real_staged[cc, h] = total[cc].astype(BF16)
        for d in y_steps:
            real_y[d] = remote(real_staged.at[ahead(c, d, n_cuts)], real_last.at[d - 1], y_peer(d))

    def real_end():
        for d in y_steps:
            real_y[d].wait_recv()
        for h in range(2):
            total = real_sum[h, c]
            for d in y_steps:
                total = total + real_last[d - 1, h].astype(F32)
            cols = slice(h * half, (h + 1) * half)
            new_ref[0, :, cols] = obj[0, :, cols] + total

    def project(angle, start):
        block = phase[angle].reshape(n_cuts * rows, pixels)
        weights = proj[pl.ds(pl.multiple_of(angle * pixels, pixels), pixels), :]
        term = dot(block, weights)
        if start:
            vol_ref[...] = term
        else:
            vol_ref[...] += term

    def to_sibling(dz, dc):
        block = block_at(dz, dc)
        s_copies[dz, dc] = remote(block, block, sibling)

    for dc in near:
        y_copies[0, dc] = remote(own, own, y_peer(dc))
    to_sibling(0, 0)
    real_begin()
    y_copies[0, opposite].wait_recv()
    to_sibling(0, opposite)
    block = block_at(0, opposite)
    for dz in close:
        far_copies[dz] = remote(block, block, z_peer(dz))
    for dz in z_steps:
        z_copies[dz].wait_recv()
        block = block_at(dz, 0)
        for dc in near if dz in close else [opposite] + near:
            y_copies[dz, dc] = remote(block, block, y_peer(dc))
        to_sibling(dz, 0)
    loads[5].wait()
    for dz in order:
        for dc in near + [opposite]:
            if dc == opposite and dz in close:
                far_copies[dz].wait_recv()
            elif (dz, dc) != (0, opposite):
                y_copies[dz, dc].wait_recv()
            if (dz, dc) != (0, opposite):
                to_sibling(dz, dc)
        project(angle_of(dz, core), dz == 0)
        if dz == order[3]:
            real_middle()
    real_end()
    for dz in order:
        for dc in range(n_cuts):
            s_copies[dz, dc].wait_recv()
        project(angle_of(dz, 1 - core), False)
    for copy in sent:
        copy.wait_send()


def hand_on(new_src, vol_src, new_ref, vol_ref, sem):
    copies = [
        pltpu.make_async_copy(new_src, new_ref, sem.at[0]),
        pltpu.make_async_copy(vol_src, vol_ref, sem.at[1]),
    ]
    for copy in copies:
        copy.start()
    for copy in copies:
        copy.wait()


def body(objects, illumination, positions, amplitudes, projector):
    n_angle, n_tile, n_cuts = (lax.axis_size(n) for n in ("angle", "tile", "cuts"))
    _, _, rows, pixels = objects.shape
    n_patch = positions.shape[1]
    width = illumination.shape[-1]
    strips = pixels // LANES
    half = pixels // 2
    pad = pixels - width
    vmem = pl.BlockSpec(memory_space=pltpu.VMEM)
    hbm = pl.BlockSpec(memory_space=pltpu.HBM)

    operands = (
        positions[0].T, objects[0], amplitudes[0], illumination, dft_table(width), projector
    )
    new_objects, volume = pl.pallas_call(
        functools.partial(kernel, n_angle, n_tile, n_cuts),
        out_shape=(
            pltpu.VMEM((2, rows, pixels), F32),
            pltpu.VMEM((n_cuts * rows, projector.shape[1]), F32),
        ),
        in_specs=[hbm] * 6,
        out_specs=(vmem, vmem),
        scratch_shapes=[
            pltpu.VMEM((2, rows, pixels), F32),
            pltpu.VMEM((n_patch, width, width), BF16),
            pltpu.VMEM((2, width, width), F32),
            pltpu.VMEM((width, 2 * width), BF16),
            pltpu.VMEM(projector.shape, BF16),
            pltpu.VMEM((2, n_tile, n_cuts, rows, pixels), BF16),
            pltpu.VMEM((2, strips, pixels, LANES), F32),
            pltpu.VMEM((2 * width, 2 * width), BF16),
            pltpu.VMEM((2 * width, 2 * width), BF16),
            pltpu.VMEM((n_patch, 2, 2 * pad + width, LANES), F32),
            pltpu.VMEM((2, 2, n_tile, n_cuts, rows, half), BF16),
            pltpu.VMEM((n_tile - 1, n_cuts, rows, half), BF16),
            pltpu.VMEM((n_cuts - 1, n_tile, rows, half), BF16),
            pltpu.VMEM((2, n_cuts, rows, half), F32),
            pltpu.VMEM((2, n_cuts, rows, half), BF16),
            pltpu.VMEM((n_tile - 1, rows, half), BF16),
            pltpu.VMEM((n_cuts - 1, rows, half), BF16),
            pltpu.VMEM((n_tile - 1, 2, n_cuts, rows, half), BF16),
            pltpu.VMEM((2, n_cuts, rows, half), F32),
            pltpu.VMEM((n_cuts, 2, rows, half), BF16),
            pltpu.VMEM((n_cuts - 1, 2, rows, half), BF16),
            pltpu.VMEM((n_angle, n_cuts, rows, pixels), BF16),
            pltpu.SMEM((2, n_patch), jnp.int32),
            pltpu.SemaphoreType.DMA((6,)),
            pltpu.SemaphoreType.DMA((COPIES,)),
            pltpu.SemaphoreType.DMA((COPIES,)),
        ],
        compiler_params=pltpu.CompilerParams(
            collective_id=0, has_side_effects=True, vmem_limit_bytes=44 * 2**20
        ),
        name="update_and_project",
    )(*(pltpu.with_memory_space_constraint(x, pltpu.HBM) for x in operands))
    any_place = pl.BlockSpec(memory_space=pl.ANY)
    new_objects, volume = pl.pallas_call(
        hand_on,
        out_shape=(
            jax.ShapeDtypeStruct(new_objects.shape, F32),
            jax.ShapeDtypeStruct(volume.shape, F32),
        ),
        in_specs=[vmem] * 2,
        out_specs=(any_place, any_place),
        scratch_shapes=[
            pltpu.SemaphoreType.DMA((2,)),
        ],
        name="hand_on",
    )(*(pltpu.with_memory_space_constraint(x, pltpu.VMEM) for x in (new_objects, volume)))
    return new_objects[None], volume


def solution(mesh):
    in_specs = (
        P("angle", None, ("tile", "cuts"), None),
        P(),
        P("angle", ("tile", "cuts"), None),
        P("angle", ("tile", "cuts"), None, None),
        P(None, ("angle", "cuts")),
    )
    out_specs = (P("angle", None, ("tile", "cuts"), None), P("tile", ("angle", "cuts")))
    return jax.shard_map(body, mesh=mesh, in_specs=in_specs, out_specs=out_specs, check_vma=False)
```

```python
import functools

import jax
import jax.numpy as jnp
import numpy as np
from jax import lax
from jax.experimental import pallas as pl
from jax.experimental.pallas import tpu as pltpu
from jax.sharding import PartitionSpec as P

MESH = pl.DeviceIdType.MESH
STEP_SIZE = 0.1
LANES = 128
CORES = 2
COPIES = 160
F32, BF16 = jnp.float32, jnp.bfloat16


def dft_table(width):
    index = np.arange(width)
    phase = (index[:, None] * index[None, :] % width) * (2.0 * np.pi / width)
    scale = 1.0 / np.sqrt(width)
    table = np.concatenate([np.cos(phase) * scale, -np.sin(phase) * scale], axis=1)
    return jnp.asarray(table.astype(np.float32)).astype(BF16)


def dot(a, b):
    return jnp.dot(a, b, preferred_element_type=F32)


def quad(a, b, c, d):
    return jnp.concatenate(
        [jnp.concatenate([a, b], axis=1), jnp.concatenate([c, d], axis=1)], axis=0
    )


def swap(x):
    w = x.shape[0] // 2
    return quad(x[:w, :w], x[w:, :w], x[:w, w:], x[w:, w:])


def near_first(n):
    return sorted(range(1, n), key=lambda d: min(d, n - d))


def kernel(
    n_angle,
    n_tile,
    n_cuts,
    pos_hbm,
    obj_hbm,
    amp_hbm,
    probe_hbm,
    table_hbm,
    proj_hbm,
    new_ref,
    vol_ref,
    obj,
    amp,
    probe,
    table,
    proj,
    bands,
    image,
    fwd,
    bwd,
    exits,
    columns,
    lines,
    terms,
    canvas,
    first_x,
    first_y,
    slab_sum,
    staged,
    last_x,
    last_y,
    real_first,
    real_sum,
    real_staged,
    real_last,
    phase,
    pos_ref,
    load_sem,
    send_sem,
    recv_sem,
):
    a, t, c = lax.axis_index("angle"), lax.axis_index("tile"), lax.axis_index("cuts")
    z, core = a // CORES, lax.rem(a, CORES)
    n_z = n_angle // CORES
    rows, pixels = obj.shape[1:]
    width = probe.shape[-1]
    strips = pixels // LANES
    half = pixels // 2
    n_patch = amp.shape[0]
    pad = pixels - width
    x_steps, y_steps, z_steps = near_first(n_tile), near_first(n_cuts), near_first(n_z)

    def ahead(at, step, n):
        return lax.rem(at + step, n)

    def behind(at, step, n):
        return lax.rem(at + n - step, n)

    def x_peer(d):
        return {"tile": ahead(t, d, n_tile)}

    def y_peer(d):
        return {"cuts": ahead(c, d, n_cuts)}

    def z_peer(d):
        return {"angle": ahead(z, d, n_z) * CORES + core}

    sibling = {"angle": z * CORES + (1 - core)}
    sent = []

    def remote(src, dst, device):
        i = len(sent)
        copy = pltpu.make_async_remote_copy(
            src_ref=src,
            dst_ref=dst,
            send_sem=send_sem.at[i],
            recv_sem=recv_sem.at[i],
            device_id=device,
            device_id_type=MESH,
        )
        copy.start()
        sent.append(copy)
        return copy

    loads = [
        pltpu.make_async_copy(src, dst, load_sem.at[i])
        for i, (src, dst) in enumerate(
            [
                (obj_hbm, obj),
                (pos_hbm, pos_ref),
                (probe_hbm, probe),
                (table_hbm, table),
                (amp_hbm, amp),
                (proj_hbm, proj),
            ]
        )
    ]
    loads[0].start()
    barrier = pltpu.get_barrier_semaphore()
    greeted = [x_peer(d) for d in x_steps] + [y_peer(d) for d in y_steps]
    greeted += [z_peer(d) for d in z_steps] + [sibling]
    for device in greeted:
        pl.semaphore_signal(barrier, inc=1, device_id=device, device_id_type=MESH)
    for load in loads[1:5]:
        load.start()
    loads[0].wait()
    for part in range(2):
        bands[part, t, c] = obj[part].astype(BF16)
    pl.semaphore_wait(barrier, len(greeted))

    first, second = {}, {}

    def go_x(part, tt, cc, key, steps=x_steps):
        for d in steps:
            block = bands.at[part, tt, cc]
            key[d] = remote(block, block, x_peer(d))

    def go_y(part, tt, cc, key, steps=y_steps):
        for d in steps:
            block = bands.at[part, tt, cc]
            key[d] = remote(block, block, y_peer(d))

    for part in range(2):
        first[part] = {}
        second[part, 0] = {}
    go_x(0, t, c, first[0])
    go_y(1, t, c, first[1])
    go_y(0, t, c, second[0, 0])
    go_x(1, t, c, second[1, 0])
    loads[5].start()

    terms_zero = jnp.zeros((pad, LANES), F32)

    @pl.loop(0, n_patch)
    def _(p):
        for part in range(2):
            terms[p, part, :pad] = terms_zero
            terms[p, part, pad + width :] = terms_zero

    loads[2].wait()
    loads[3].wait()
    f_re, f_im = table[:, :width], table[:, width:]
    fwd[...] = quad(f_re, f_im, -f_im, f_re)
    bwd[...] = quad(f_re, -f_im, f_im, f_re)

    def unpack(part, tt, cc):
        at = pl.ds(pl.multiple_of((tt * n_cuts + cc) * rows, rows), rows)
        block = bands[part, tt, cc]
        for j in range(strips):
            image[part, j, at, :] = block[:, j * LANES : (j + 1) * LANES].astype(F32)

    unpack(0, t, c)
    unpack(1, t, c)
    x_far, y_far = n_tile // 2, n_cuts // 2
    x_near, y_near = [d for d in x_steps if d != x_far], [d for d in y_steps if d != y_far]
    turned = {}

    def back_x(d):
        return behind(t, d, n_tile)

    def back_y(d):
        return behind(c, d, n_cuts)

    for dx, dy in zip(x_near, y_near):
        first[0][dx].wait_recv()
        second[0, dx] = {}
        go_y(0, back_x(dx), c, second[0, dx], y_near)
        first[1][dy].wait_recv()
        second[1, dy] = {}
        go_x(1, t, back_y(dy), second[1, dy], x_near)
    first[0][x_far].wait_recv()
    second[0, x_far] = {}
    go_y(0, back_x(x_far), c, second[0, x_far])
    first[1][y_far].wait_recv()
    second[1, y_far] = {}
    go_x(1, t, back_y(y_far), second[1, y_far])
    second[0, 0][y_far].wait_recv()
    turned[0] = {}
    go_x(0, t, back_y(y_far), turned[0], x_near)
    second[1, 0][x_far].wait_recv()
    turned[1] = {}
    go_y(1, back_x(x_far), c, turned[1], y_near)
    for d in x_steps:
        unpack(0, back_x(d), c)
    for d in y_steps:
        unpack(1, t, back_y(d))
    unpack(0, t, back_y(y_far))
    unpack(1, back_x(x_far), c)
    for d in [0] + x_near + [x_far]:
        for e in y_near + [y_far] * (d == x_far):
            second[0, d][e].wait_recv()
            unpack(0, back_x(d), back_y(e))
    for d in [0] + y_near + [y_far]:
        for e in x_near + [x_far] * (d == y_far):
            second[1, d][e].wait_recv()
            unpack(1, back_x(e), back_y(d))
    for d in x_near:
        turned[0][d].wait_recv()
        unpack(0, back_x(d), back_y(y_far))
    for d in y_near:
        turned[1][d].wait_recv()
        unpack(1, back_x(x_far), back_y(d))
    loads[4].wait()
    loads[1].wait()

    lane = lax.broadcasted_iota(jnp.int32, (width, LANES), 1)

    def spread_pair(i, carry):
        found = []
        p_re, p_im = probe[0], probe[1]
        for k in range(2):
            row, col = pos_ref[0, 2 * i + k], pos_ref[1, 2 * i + k]
            strip, shift = col // LANES, lax.rem(col, LANES)

            def window(part):
                left = image[part, strip, pl.ds(row, width), :]
                right = image[part, jnp.minimum(strip + 1, strips - 1), pl.ds(row, width), :]
                joined = jnp.where(lane >= shift, left, right)
                return pltpu.roll(joined, lax.rem(LANES - shift, LANES), 1)

            w_re, w_im = window(0), window(1)
            e_re, e_im = p_re * w_re - p_im * w_im, p_re * w_im + p_im * w_re
            exits[2 * i + k, 0] = e_re
            exits[2 * i + k, 1] = e_im
            found.append((e_re, e_im))
        columns[i] = swap(dot(quad(*found[0], *found[1]).astype(BF16), fwd[...]).astype(BF16))
        return carry

    def project_pair(i, carry):
        spectrum = dot(bwd[...], columns[i])
        s_re, s_im = spectrum[:width], spectrum[width:]
        measured = jnp.concatenate([amp[2 * i], amp[2 * i + 1]], axis=1).astype(F32)
        scaling = measured * lax.rsqrt(jnp.maximum(s_re * s_re + s_im * s_im, 1.0))
        projected = jnp.concatenate([s_re * scaling, s_im * scaling], axis=0)
        lines[i] = swap(projected.astype(BF16))
        return carry

    def back_pair(i, carry):
        columns[i] = swap(dot(lines[i], bwd[...]).astype(BF16))
        return carry

    def term_pair(i, carry):
        revised = dot(fwd[...], columns[i])
        p_re, p_im = probe[0], probe[1]
        for k in range(2):
            shift = lax.rem(pos_ref[1, 2 * i + k], LANES)
            cols = slice(k * width, (k + 1) * width)
            d_re = revised[:width, cols] - exits[2 * i + k, 0]
            d_im = revised[width:, cols] - exits[2 * i + k, 1]
            u_re = STEP_SIZE * (p_re * d_re + p_im * d_im)
            u_im = STEP_SIZE * (p_re * d_im - p_im * d_re)
            terms[2 * i + k, 0, pad : pad + width] = pltpu.roll(u_re, shift, 1)
            terms[2 * i + k, 1, pad : pad + width] = pltpu.roll(u_im, shift, 1)
        return carry

    for stage in (spread_pair, project_pair, back_pair, term_pair):
        lax.fori_loop(0, n_patch // 2, stage, 0, unroll=True)

    piece = 64
    lane8 = lax.broadcasted_iota(jnp.int32, (8, LANES), 1)

    pieces = n_cuts * rows // piece

    def build(part, slab, which):
        for q in which:
            base = pad + slab * (n_cuts * rows) + q * piece

            def add(p, totals):
                row, col = pos_ref[0, p], pos_ref[1, p]
                strip, shift = col // LANES, lax.rem(col, LANES)
                block = terms[p, part, pl.ds(base - row, piece), :].reshape(piece // 8, 8, LANES)
                place = strip + jnp.where(lane8 < shift, 1, 0)
                return tuple(
                    total + jnp.where((place == j)[None], block, 0.0)
                    for j, total in enumerate(totals)
                )

            zero = jnp.zeros((piece // 8, 8, LANES), F32)
            totals = lax.fori_loop(0, n_patch, add, (zero,) * strips, unroll=True)
            for h in range(2):
                wide = jnp.concatenate(
                    [x.reshape(piece, LANES) for x in totals[h * strips // 2 : (h + 1) * strips // 2]],
                    axis=1,
                ).astype(BF16)
                for b in range(piece // rows):
                    canvas[part, h, slab, q * (piece // rows) + b] = wide[b * rows : (b + 1) * rows]

    sum_x, sum_y = {}, {}
    pair_size = piece // rows
    mine, odd = c // pair_size, lax.rem(c, pair_size)
    partner = {1: c + 1 - 2 * odd, 2: ahead(c, 2, n_cuts), 3: n_cuts - 1 - c}
    for turn, q in enumerate((1 - mine, mine)):
        part_rows = pl.ds(q * pair_size, pair_size)
        for d in x_steps[::-1] + [0]:
            slab = ahead(t, d, n_tile)
            build(1, slab, [q])
            if d:
                sum_x[d, turn] = remote(
                    canvas.at[1, 0, slab, part_rows], first_x.at[d - 1, part_rows], x_peer(d)
                )
        for m in (2, 3) if turn == 0 else (1,):
            sum_y[m] = remote(
                canvas.at[1, 1, :, partner[m]], first_y.at[m - 1], {"cuts": partner[m]}
            )
    for slab in range(n_tile):
        build(0, slab, range(pieces))

    fin_x, fin_y = {}, {}
    for d in x_steps:
        for turn in range(2):
            sum_x[d, turn].wait_recv()
    total = canvas[1, 0, t].astype(F32)
    for d in x_steps:
        total = total + first_x[d - 1].astype(F32)
    slab_sum[0] = total
    staged[0] = total.astype(BF16)
    for d in reversed(y_steps):
        fin_y[d] = remote(staged.at[0, ahead(c, d, n_cuts)], last_y.at[d - 1], y_peer(d))
    for d in y_steps:
        sum_y[d].wait_recv()
    for tt in range(n_tile):
        total = canvas[1, 1, tt, c].astype(F32)
        for d in y_steps:
            total = total + first_y[d - 1, tt].astype(F32)
        slab_sum[1, tt] = total
        staged[1, tt] = total.astype(BF16)
    for d in reversed(x_steps):
        fin_x[d] = remote(staged.at[1, ahead(t, d, n_tile)], last_x.at[d - 1], x_peer(d))
    for d in y_steps:
        fin_y[d].wait_recv()
    left = slab_sum[0, c]
    for d in y_steps:
        left = left + last_y[d - 1].astype(F32)
    for d in x_steps:
        fin_x[d].wait_recv()
    right = slab_sum[1, t]
    for d in x_steps:
        right = right + last_x[d - 1].astype(F32)
    update = jnp.concatenate([left, right], axis=1)
    phase[a, c] = (bands[1, t, c].astype(F32) + update).astype(BF16)
    new_ref[1] = obj[1] + update

    z_copies, y_copies, far_copies, s_copies = {}, {}, {}, {}
    order = [0] + z_steps
    opposite = n_cuts // 2
    near = [1, n_cuts - 1]
    close = z_steps[:4]

    def angle_of(dz, which):
        return behind(z, dz, n_z) * CORES + which

    def block_at(dz, dc):
        return phase.at[angle_of(dz, core), behind(c, dc, n_cuts)]

    own = block_at(0, 0)
    y_copies[0, opposite] = remote(own, own, y_peer(opposite))
    for dz in z_steps:
        z_copies[dz] = remote(own, own, z_peer(dz))

    real_x, real_y = {}, {}

    def real_begin():
        for d in reversed(x_steps):
            real_x[d] = remote(
                canvas.at[0, :, ahead(t, d, n_tile)], real_first.at[d - 1], x_peer(d)
            )

    def real_middle():
        for d in x_steps:
            real_x[d].wait_recv()
        for h in range(2):
            total = canvas[0, h, t].astype(F32)
            for d in x_steps:
                total = total + real_first[d - 1, h].astype(F32)
            real_sum[h] = total
            for cc in range(n_cuts):
                real_staged[cc, h] = total[cc].astype(BF16)
        for d in y_steps:
            real_y[d] = remote(real_staged.at[ahead(c, d, n_cuts)], real_last.at[d - 1], y_peer(d))

    def real_end():
        for d in y_steps:
            real_y[d].wait_recv()
        for h in range(2):
            total = real_sum[h, c]
            for d in y_steps:
                total = total + real_last[d - 1, h].astype(F32)
            cols = slice(h * half, (h + 1) * half)
            new_ref[0, :, cols] = obj[0, :, cols] + total

    def project(angle, start):
        block = phase[angle].reshape(n_cuts * rows, pixels)
        weights = proj[pl.ds(pl.multiple_of(angle * pixels, pixels), pixels), :]
        term = dot(block, weights)
        if start:
            vol_ref[...] = term
        else:
            vol_ref[...] += term

    def to_sibling(dz, dc):
        block = block_at(dz, dc)
        s_copies[dz, dc] = remote(block, block, sibling)

    for dc in near:
        y_copies[0, dc] = remote(own, own, y_peer(dc))
    to_sibling(0, 0)
    real_begin()
    y_copies[0, opposite].wait_recv()
    to_sibling(0, opposite)
    block = block_at(0, opposite)
    for dz in close:
        far_copies[dz] = remote(block, block, z_peer(dz))
    for dz in z_steps:
        z_copies[dz].wait_recv()
        block = block_at(dz, 0)
        for dc in near if dz in close else [opposite] + near:
            y_copies[dz, dc] = remote(block, block, y_peer(dc))
        to_sibling(dz, 0)
    loads[5].wait()
    for dz in order:
        for dc in near + [opposite]:
            if dc == opposite and dz in close:
                far_copies[dz].wait_recv()
            elif (dz, dc) != (0, opposite):
                y_copies[dz, dc].wait_recv()
            if (dz, dc) != (0, opposite):
                to_sibling(dz, dc)
        project(angle_of(dz, core), dz == 0)
        if dz == order[3]:
            real_middle()
    real_end()
    for dz in order:
        for dc in range(n_cuts):
            s_copies[dz, dc].wait_recv()
        project(angle_of(dz, 1 - core), False)
    for copy in sent:
        copy.wait_send()


def hand_on(new_src, vol_src, new_ref, vol_ref, sem):
    copies = [
        pltpu.make_async_copy(new_src, new_ref, sem.at[0]),
        pltpu.make_async_copy(vol_src, vol_ref, sem.at[1]),
    ]
    for copy in copies:
        copy.start()
    for copy in copies:
        copy.wait()


def body(objects, illumination, positions, amplitudes, projector):
    n_angle, n_tile, n_cuts = (lax.axis_size(n) for n in ("angle", "tile", "cuts"))
    _, _, rows, pixels = objects.shape
    n_patch = positions.shape[1]
    width = illumination.shape[-1]
    strips = pixels // LANES
    half = pixels // 2
    pad = pixels - width
    vmem = pl.BlockSpec(memory_space=pltpu.VMEM)
    hbm = pl.BlockSpec(memory_space=pltpu.HBM)

    operands = (
        positions[0].T, objects[0], amplitudes[0], illumination, dft_table(width), projector
    )
    new_objects, volume = pl.pallas_call(
        functools.partial(kernel, n_angle, n_tile, n_cuts),
        out_shape=(
            pltpu.VMEM((2, rows, pixels), F32),
            pltpu.VMEM((n_cuts * rows, projector.shape[1]), F32),
        ),
        in_specs=[hbm] * 6,
        out_specs=(vmem, vmem),
        scratch_shapes=[
            pltpu.VMEM((2, rows, pixels), F32),
            pltpu.VMEM((n_patch, width, width), BF16),
            pltpu.VMEM((2, width, width), F32),
            pltpu.VMEM((width, 2 * width), BF16),
            pltpu.VMEM(projector.shape, BF16),
            pltpu.VMEM((2, n_tile, n_cuts, rows, pixels), BF16),
            pltpu.VMEM((2, strips, pixels, LANES), F32),
            pltpu.VMEM((2 * width, 2 * width), BF16),
            pltpu.VMEM((2 * width, 2 * width), BF16),
            pltpu.VMEM((n_patch, 2, width, width), F32),
            pltpu.VMEM((n_patch // 2, 2 * width, 2 * width), BF16),
            pltpu.VMEM((n_patch // 2, 2 * width, 2 * width), BF16),
            pltpu.VMEM((n_patch, 2, 2 * pad + width, LANES), F32),
            pltpu.VMEM((2, 2, n_tile, n_cuts, rows, half), BF16),
            pltpu.VMEM((n_tile - 1, n_cuts, rows, half), BF16),
            pltpu.VMEM((n_cuts - 1, n_tile, rows, half), BF16),
            pltpu.VMEM((2, n_cuts, rows, half), F32),
            pltpu.VMEM((2, n_cuts, rows, half), BF16),
            pltpu.VMEM((n_tile - 1, rows, half), BF16),
            pltpu.VMEM((n_cuts - 1, rows, half), BF16),
            pltpu.VMEM((n_tile - 1, 2, n_cuts, rows, half), BF16),
            pltpu.VMEM((2, n_cuts, rows, half), F32),
            pltpu.VMEM((n_cuts, 2, rows, half), BF16),
            pltpu.VMEM((n_cuts - 1, 2, rows, half), BF16),
            pltpu.VMEM((n_angle, n_cuts, rows, pixels), BF16),
            pltpu.SMEM((2, n_patch), jnp.int32),
            pltpu.SemaphoreType.DMA((6,)),
            pltpu.SemaphoreType.DMA((COPIES,)),
            pltpu.SemaphoreType.DMA((COPIES,)),
        ],
        compiler_params=pltpu.CompilerParams(
            collective_id=0, has_side_effects=True, vmem_limit_bytes=44 * 2**20
        ),
        name="update_and_project",
    )(*(pltpu.with_memory_space_constraint(x, pltpu.HBM) for x in operands))
    any_place = pl.BlockSpec(memory_space=pl.ANY)
    new_objects, volume = pl.pallas_call(
        hand_on,
        out_shape=(
            jax.ShapeDtypeStruct(new_objects.shape, F32),
            jax.ShapeDtypeStruct(volume.shape, F32),
        ),
        in_specs=[vmem] * 2,
        out_specs=(any_place, any_place),
        scratch_shapes=[
            pltpu.SemaphoreType.DMA((2,)),
        ],
        name="hand_on",
    )(*(pltpu.with_memory_space_constraint(x, pltpu.VMEM) for x in (new_objects, volume)))
    return new_objects[None], volume


def solution(mesh):
    in_specs = (
        P("angle", None, ("tile", "cuts"), None),
        P(),
        P("angle", ("tile", "cuts"), None),
        P("angle", ("tile", "cuts"), None, None),
        P(None, ("angle", "cuts")),
    )
    out_specs = (P("angle", None, ("tile", "cuts"), None), P("tile", ("angle", "cuts")))
    return jax.shard_map(body, mesh=mesh, in_specs=in_specs, out_specs=out_specs, check_vma=False)
```

```python
import functools

import jax
import jax.numpy as jnp
import numpy as np
from jax import lax
from jax.experimental import pallas as pl
from jax.experimental.pallas import tpu as pltpu
from jax.sharding import PartitionSpec as P

MESH = pl.DeviceIdType.MESH
STEP_SIZE = 0.1
LANES = 128
CORES = 2
COPIES = 160
F32, BF16 = jnp.float32, jnp.bfloat16


def dft_table(width):
    index = np.arange(width)
    phase = (index[:, None] * index[None, :] % width) * (2.0 * np.pi / width)
    scale = 1.0 / np.sqrt(width)
    table = np.concatenate([np.cos(phase) * scale, -np.sin(phase) * scale], axis=1)
    return jnp.asarray(table.astype(np.float32)).astype(BF16)


def dot(a, b):
    return jnp.dot(a, b, preferred_element_type=F32)


def quad(a, b, c, d):
    return jnp.concatenate(
        [jnp.concatenate([a, b], axis=1), jnp.concatenate([c, d], axis=1)], axis=0
    )


def swap(x):
    w = x.shape[0] // 2
    return quad(x[:w, :w], x[w:, :w], x[:w, w:], x[w:, w:])


def near_first(n):
    return sorted(range(1, n), key=lambda d: min(d, n - d))


def kernel(
    n_angle,
    n_tile,
    n_cuts,
    pos_hbm,
    obj_hbm,
    amp_hbm,
    probe_hbm,
    table_hbm,
    proj_hbm,
    new_ref,
    vol_ref,
    obj,
    amp,
    probe,
    table,
    proj,
    bands,
    image,
    fwd,
    bwd,
    exits,
    columns,
    lines,
    terms,
    canvas,
    first_x,
    first_y,
    slab_sum,
    staged,
    last_x,
    last_y,
    real_first,
    real_sum,
    real_staged,
    real_last,
    phase,
    pos_ref,
    load_sem,
    send_sem,
    recv_sem,
):
    a, t, c = lax.axis_index("angle"), lax.axis_index("tile"), lax.axis_index("cuts")
    z, core = a // CORES, lax.rem(a, CORES)
    n_z = n_angle // CORES
    rows, pixels = obj.shape[1:]
    width = probe.shape[-1]
    strips = pixels // LANES
    half = pixels // 2
    n_patch = amp.shape[0]
    pad = pixels - width
    x_steps, y_steps, z_steps = near_first(n_tile), near_first(n_cuts), near_first(n_z)

    def ahead(at, step, n):
        return lax.rem(at + step, n)

    def behind(at, step, n):
        return lax.rem(at + n - step, n)

    def x_peer(d):
        return {"tile": ahead(t, d, n_tile)}

    def y_peer(d):
        return {"cuts": ahead(c, d, n_cuts)}

    def z_peer(d):
        return {"angle": ahead(z, d, n_z) * CORES + core}

    sibling = {"angle": z * CORES + (1 - core)}
    sent = []

    def remote(src, dst, device):
        i = len(sent)
        copy = pltpu.make_async_remote_copy(
            src_ref=src,
            dst_ref=dst,
            send_sem=send_sem.at[i],
            recv_sem=recv_sem.at[i],
            device_id=device,
            device_id_type=MESH,
        )
        copy.start()
        sent.append(copy)
        return copy

    loads = [
        pltpu.make_async_copy(src, dst, load_sem.at[i])
        for i, (src, dst) in enumerate(
            [
                (obj_hbm, obj),
                (pos_hbm, pos_ref),
                (probe_hbm, probe),
                (table_hbm, table),
                (amp_hbm, amp),
                (proj_hbm, proj),
            ]
        )
    ]
    loads[0].start()
    barrier = pltpu.get_barrier_semaphore()
    greeted = [x_peer(d) for d in x_steps] + [y_peer(d) for d in y_steps]
    greeted += [z_peer(d) for d in z_steps] + [sibling]
    for device in greeted:
        pl.semaphore_signal(barrier, inc=1, device_id=device, device_id_type=MESH)
    for load in loads[1:5]:
        load.start()
    loads[0].wait()
    for part in range(2):
        bands[part, t, c] = obj[part].astype(BF16)
    pl.semaphore_wait(barrier, len(greeted))

    first, second = {}, {}

    def go_x(part, tt, cc, key, steps=x_steps):
        for d in steps:
            block = bands.at[part, tt, cc]
            key[d] = remote(block, block, x_peer(d))

    def go_y(part, tt, cc, key, steps=y_steps):
        for d in steps:
            block = bands.at[part, tt, cc]
            key[d] = remote(block, block, y_peer(d))

    for part in range(2):
        first[part] = {}
        second[part, 0] = {}
    go_x(0, t, c, first[0])
    go_y(1, t, c, first[1])
    go_y(0, t, c, second[0, 0])
    go_x(1, t, c, second[1, 0])
    loads[5].start()

    terms_zero = jnp.zeros((pad, LANES), F32)

    @pl.loop(0, n_patch)
    def _(p):
        for part in range(2):
            terms[p, part, :pad] = terms_zero
            terms[p, part, pad + width :] = terms_zero

    loads[2].wait()
    loads[3].wait()
    f_re, f_im = table[:, :width], table[:, width:]
    fwd[...] = quad(f_re, f_im, -f_im, f_re)
    bwd[...] = quad(f_re, -f_im, f_im, f_re)

    def unpack(part, tt, cc):
        at = pl.ds(pl.multiple_of((tt * n_cuts + cc) * rows, rows), rows)
        block = bands[part, tt, cc]
        for j in range(strips):
            image[part, j, at, :] = block[:, j * LANES : (j + 1) * LANES].astype(F32)

    unpack(0, t, c)
    unpack(1, t, c)
    x_far, y_far = n_tile // 2, n_cuts // 2
    x_near, y_near = [d for d in x_steps if d != x_far], [d for d in y_steps if d != y_far]
    turned = {}

    def back_x(d):
        return behind(t, d, n_tile)

    def back_y(d):
        return behind(c, d, n_cuts)

    for dx, dy in zip(x_near, y_near):
        first[0][dx].wait_recv()
        second[0, dx] = {}
        go_y(0, back_x(dx), c, second[0, dx], y_near)
        first[1][dy].wait_recv()
        second[1, dy] = {}
        go_x(1, t, back_y(dy), second[1, dy], x_near)
    first[0][x_far].wait_recv()
    second[0, x_far] = {}
    go_y(0, back_x(x_far), c, second[0, x_far])
    first[1][y_far].wait_recv()
    second[1, y_far] = {}
    go_x(1, t, back_y(y_far), second[1, y_far])
    second[0, 0][y_far].wait_recv()
    turned[0] = {}
    go_x(0, t, back_y(y_far), turned[0], x_near)
    second[1, 0][x_far].wait_recv()
    turned[1] = {}
    go_y(1, back_x(x_far), c, turned[1], y_near)
    for d in x_steps:
        unpack(0, back_x(d), c)
    for d in y_steps:
        unpack(1, t, back_y(d))
    unpack(0, t, back_y(y_far))
    unpack(1, back_x(x_far), c)
    for d in [0] + x_near + [x_far]:
        for e in y_near + [y_far] * (d == x_far):
            second[0, d][e].wait_recv()
            unpack(0, back_x(d), back_y(e))
    for d in [0] + y_near + [y_far]:
        for e in x_near + [x_far] * (d == y_far):
            second[1, d][e].wait_recv()
            unpack(1, back_x(e), back_y(d))
    for d in x_near:
        turned[0][d].wait_recv()
        unpack(0, back_x(d), back_y(y_far))
    for d in y_near:
        turned[1][d].wait_recv()
        unpack(1, back_x(x_far), back_y(d))
    loads[4].wait()
    loads[1].wait()

    lane = lax.broadcasted_iota(jnp.int32, (width, LANES), 1)

    def spread_pair(i, carry):
        found = []
        p_re, p_im = probe[0], probe[1]
        for k in range(2):
            row, col = pos_ref[0, 2 * i + k], pos_ref[1, 2 * i + k]
            strip, shift = col // LANES, lax.rem(col, LANES)

            def window(part):
                left = image[part, strip, pl.ds(row, width), :]
                right = image[part, jnp.minimum(strip + 1, strips - 1), pl.ds(row, width), :]
                joined = jnp.where(lane >= shift, left, right)
                return pltpu.roll(joined, lax.rem(LANES - shift, LANES), 1)

            w_re, w_im = window(0), window(1)
            e_re, e_im = p_re * w_re - p_im * w_im, p_re * w_im + p_im * w_re
            exits[2 * i + k, 0] = e_re
            exits[2 * i + k, 1] = e_im
            found.append((e_re, e_im))
        columns[i] = swap(dot(quad(*found[0], *found[1]).astype(BF16), fwd[...]).astype(BF16))
        return carry

    def project_pair(i, carry):
        spectrum = dot(bwd[...], columns[i])
        s_re, s_im = spectrum[:width], spectrum[width:]
        measured = jnp.concatenate([amp[2 * i], amp[2 * i + 1]], axis=1).astype(F32)
        scaling = measured * lax.rsqrt(jnp.maximum(s_re * s_re + s_im * s_im, 1.0))
        projected = jnp.concatenate([s_re * scaling, s_im * scaling], axis=0)
        lines[i] = swap(projected.astype(BF16))
        return carry

    def back_pair(i, carry):
        columns[i] = swap(dot(lines[i], bwd[...]).astype(BF16))
        return carry

    def term_pair(i, carry):
        revised = dot(fwd[...], columns[i])
        p_re, p_im = probe[0], probe[1]
        for k in range(2):
            shift = lax.rem(pos_ref[1, 2 * i + k], LANES)
            cols = slice(k * width, (k + 1) * width)
            d_re = revised[:width, cols] - exits[2 * i + k, 0]
            d_im = revised[width:, cols] - exits[2 * i + k, 1]
            u_re = STEP_SIZE * (p_re * d_re + p_im * d_im)
            u_im = STEP_SIZE * (p_re * d_im - p_im * d_re)
            terms[2 * i + k, 0, pad : pad + width] = pltpu.roll(u_re, shift, 1)
            terms[2 * i + k, 1, pad : pad + width] = pltpu.roll(u_im, shift, 1)
        return carry

    for stage in (spread_pair, project_pair, back_pair, term_pair):
        lax.fori_loop(0, n_patch // 2, stage, 0, unroll=True)

    piece = 64
    lane8 = lax.broadcasted_iota(jnp.int32, (8, LANES), 1)

    pieces = n_cuts * rows // piece

    def build(part, slab, which):
        for q in which:
            base = pad + slab * (n_cuts * rows) + q * piece

            def add(p, totals):
                row, col = pos_ref[0, p], pos_ref[1, p]
                strip, shift = col // LANES, lax.rem(col, LANES)
                block = terms[p, part, pl.ds(base - row, piece), :].reshape(piece // 8, 8, LANES)
                place = strip + jnp.where(lane8 < shift, 1, 0)
                return tuple(
                    total + jnp.where((place == j)[None], block, 0.0)
                    for j, total in enumerate(totals)
                )

            zero = jnp.zeros((piece // 8, 8, LANES), F32)
            totals = lax.fori_loop(0, n_patch, add, (zero,) * strips, unroll=True)
            for h in range(2):
                wide = jnp.concatenate(
                    [x.reshape(piece, LANES) for x in totals[h * strips // 2 : (h + 1) * strips // 2]],
                    axis=1,
                ).astype(BF16)
                for b in range(piece // rows):
                    canvas[part, h, slab, q * (piece // rows) + b] = wide[b * rows : (b + 1) * rows]

    sum_x, sum_y = {}, {}
    pair_size = piece // rows
    mine, odd = c // pair_size, lax.rem(c, pair_size)
    partner = {1: c + 1 - 2 * odd, 2: ahead(c, 2, n_cuts), 3: n_cuts - 1 - c}
    for turn, q in enumerate((1 - mine, mine)):
        part_rows = pl.ds(q * pair_size, pair_size)
        for d in x_steps[::-1] + [0]:
            slab = ahead(t, d, n_tile)
            build(1, slab, [q])
            if d:
                sum_x[d, turn] = remote(
                    canvas.at[1, 0, slab, part_rows], first_x.at[d - 1, part_rows], x_peer(d)
                )
        for m in (2, 3) if turn == 0 else (1,):
            sum_y[m] = remote(
                canvas.at[1, 1, :, partner[m]], first_y.at[m - 1], {"cuts": partner[m]}
            )
    for slab in range(n_tile):
        build(0, slab, range(pieces))

    fin_x, fin_y = {}, {}
    for d in x_steps:
        for turn in range(2):
            sum_x[d, turn].wait_recv()
    total = canvas[1, 0, t].astype(F32)
    for d in x_steps:
        total = total + first_x[d - 1].astype(F32)
    slab_sum[0] = total
    staged[0] = total.astype(BF16)
    for d in reversed(y_steps):
        fin_y[d] = remote(staged.at[0, ahead(c, d, n_cuts)], last_y.at[d - 1], y_peer(d))
    for d in y_steps:
        sum_y[d].wait_recv()
    for tt in range(n_tile):
        total = canvas[1, 1, tt, c].astype(F32)
        for d in y_steps:
            total = total + first_y[d - 1, tt].astype(F32)
        slab_sum[1, tt] = total
        staged[1, tt] = total.astype(BF16)
    for d in reversed(x_steps):
        fin_x[d] = remote(staged.at[1, ahead(t, d, n_tile)], last_x.at[d - 1], x_peer(d))
    for d in y_steps:
        fin_y[d].wait_recv()
    left = slab_sum[0, c]
    for d in y_steps:
        left = left + last_y[d - 1].astype(F32)
    for d in x_steps:
        fin_x[d].wait_recv()
    right = slab_sum[1, t]
    for d in x_steps:
        right = right + last_x[d - 1].astype(F32)
    update = jnp.concatenate([left, right], axis=1)
    phase[a, c] = (bands[1, t, c].astype(F32) + update).astype(BF16)
    new_ref[1] = obj[1] + update

    z_copies, y_copies, far_copies, s_copies = {}, {}, {}, {}
    order = [0] + z_steps
    opposite = n_cuts // 2
    near = [1, n_cuts - 1]
    close = z_steps[:4]

    def angle_of(dz, which):
        return behind(z, dz, n_z) * CORES + which

    def block_at(dz, dc):
        return phase.at[angle_of(dz, core), behind(c, dc, n_cuts)]

    own = block_at(0, 0)
    y_copies[0, opposite] = remote(own, own, y_peer(opposite))
    for dz in z_steps:
        z_copies[dz] = remote(own, own, z_peer(dz))

    real_x, real_y = {}, {}

    def real_begin():
        for d in reversed(x_steps):
            real_x[d] = remote(
                canvas.at[0, :, ahead(t, d, n_tile)], real_first.at[d - 1], x_peer(d)
            )

    def real_middle():
        for d in x_steps:
            real_x[d].wait_recv()
        for h in range(2):
            total = canvas[0, h, t].astype(F32)
            for d in x_steps:
                total = total + real_first[d - 1, h].astype(F32)
            real_sum[h] = total
            for cc in range(n_cuts):
                real_staged[cc, h] = total[cc].astype(BF16)
        for d in y_steps:
            real_y[d] = remote(real_staged.at[ahead(c, d, n_cuts)], real_last.at[d - 1], y_peer(d))

    def real_end():
        for d in y_steps:
            real_y[d].wait_recv()
        for h in range(2):
            total = real_sum[h, c]
            for d in y_steps:
                total = total + real_last[d - 1, h].astype(F32)
            cols = slice(h * half, (h + 1) * half)
            new_ref[0, :, cols] = obj[0, :, cols] + total

    def project(angle, start):
        block = phase[angle].reshape(n_cuts * rows, pixels)
        weights = proj[pl.ds(pl.multiple_of(angle * pixels, pixels), pixels), :]
        term = dot(block, weights)
        if start:
            vol_ref[...] = term
        else:
            vol_ref[...] += term

    def to_sibling(dz, dc):
        block = block_at(dz, dc)
        s_copies[dz, dc] = remote(block, block, sibling)

    for dc in near:
        y_copies[0, dc] = remote(own, own, y_peer(dc))
    to_sibling(0, 0)
    y_copies[0, opposite].wait_recv()
    to_sibling(0, opposite)
    block = block_at(0, opposite)
    for dz in close:
        far_copies[dz] = remote(block, block, z_peer(dz))
    real_begin()
    for dz in z_steps:
        z_copies[dz].wait_recv()
        block = block_at(dz, 0)
        for dc in near if dz in close else [opposite] + near:
            y_copies[dz, dc] = remote(block, block, y_peer(dc))
        to_sibling(dz, 0)
    loads[5].wait()
    for dz in order:
        for dc in near + [opposite]:
            if dc == opposite and dz in close:
                far_copies[dz].wait_recv()
            elif (dz, dc) != (0, opposite):
                y_copies[dz, dc].wait_recv()
            if (dz, dc) != (0, opposite):
                to_sibling(dz, dc)
        project(angle_of(dz, core), dz == 0)
        if dz == order[3]:
            real_middle()
    real_end()
    for dz in order:
        for dc in range(n_cuts):
            s_copies[dz, dc].wait_recv()
        project(angle_of(dz, 1 - core), False)
    for copy in sent:
        copy.wait_send()


def hand_on(new_src, vol_src, new_ref, vol_ref, sem):
    copies = [
        pltpu.make_async_copy(new_src, new_ref, sem.at[0]),
        pltpu.make_async_copy(vol_src, vol_ref, sem.at[1]),
    ]
    for copy in copies:
        copy.start()
    for copy in copies:
        copy.wait()


def body(objects, illumination, positions, amplitudes, projector):
    n_angle, n_tile, n_cuts = (lax.axis_size(n) for n in ("angle", "tile", "cuts"))
    _, _, rows, pixels = objects.shape
    n_patch = positions.shape[1]
    width = illumination.shape[-1]
    strips = pixels // LANES
    half = pixels // 2
    pad = pixels - width
    vmem = pl.BlockSpec(memory_space=pltpu.VMEM)
    hbm = pl.BlockSpec(memory_space=pltpu.HBM)

    operands = (
        positions[0].T, objects[0], amplitudes[0], illumination, dft_table(width), projector
    )
    new_objects, volume = pl.pallas_call(
        functools.partial(kernel, n_angle, n_tile, n_cuts),
        out_shape=(
            pltpu.VMEM((2, rows, pixels), F32),
            pltpu.VMEM((n_cuts * rows, projector.shape[1]), F32),
        ),
        in_specs=[hbm] * 6,
        out_specs=(vmem, vmem),
        scratch_shapes=[
            pltpu.VMEM((2, rows, pixels), F32),
            pltpu.VMEM((n_patch, width, width), BF16),
            pltpu.VMEM((2, width, width), F32),
            pltpu.VMEM((width, 2 * width), BF16),
            pltpu.VMEM(projector.shape, BF16),
            pltpu.VMEM((2, n_tile, n_cuts, rows, pixels), BF16),
            pltpu.VMEM((2, strips, pixels, LANES), F32),
            pltpu.VMEM((2 * width, 2 * width), BF16),
            pltpu.VMEM((2 * width, 2 * width), BF16),
            pltpu.VMEM((n_patch, 2, width, width), F32),
            pltpu.VMEM((n_patch // 2, 2 * width, 2 * width), BF16),
            pltpu.VMEM((n_patch // 2, 2 * width, 2 * width), BF16),
            pltpu.VMEM((n_patch, 2, 2 * pad + width, LANES), F32),
            pltpu.VMEM((2, 2, n_tile, n_cuts, rows, half), BF16),
            pltpu.VMEM((n_tile - 1, n_cuts, rows, half), BF16),
            pltpu.VMEM((n_cuts - 1, n_tile, rows, half), BF16),
            pltpu.VMEM((2, n_cuts, rows, half), F32),
            pltpu.VMEM((2, n_cuts, rows, half), BF16),
            pltpu.VMEM((n_tile - 1, rows, half), BF16),
            pltpu.VMEM((n_cuts - 1, rows, half), BF16),
            pltpu.VMEM((n_tile - 1, 2, n_cuts, rows, half), BF16),
            pltpu.VMEM((2, n_cuts, rows, half), F32),
            pltpu.VMEM((n_cuts, 2, rows, half), BF16),
            pltpu.VMEM((n_cuts - 1, 2, rows, half), BF16),
            pltpu.VMEM((n_angle, n_cuts, rows, pixels), BF16),
            pltpu.SMEM((2, n_patch), jnp.int32),
            pltpu.SemaphoreType.DMA((6,)),
            pltpu.SemaphoreType.DMA((COPIES,)),
            pltpu.SemaphoreType.DMA((COPIES,)),
        ],
        compiler_params=pltpu.CompilerParams(
            collective_id=0, has_side_effects=True, vmem_limit_bytes=44 * 2**20
        ),
        name="update_and_project",
    )(*(pltpu.with_memory_space_constraint(x, pltpu.HBM) for x in operands))
    any_place = pl.BlockSpec(memory_space=pl.ANY)
    new_objects, volume = pl.pallas_call(
        hand_on,
        out_shape=(
            jax.ShapeDtypeStruct(new_objects.shape, F32),
            jax.ShapeDtypeStruct(volume.shape, F32),
        ),
        in_specs=[vmem] * 2,
        out_specs=(any_place, any_place),
        scratch_shapes=[
            pltpu.SemaphoreType.DMA((2,)),
        ],
        name="hand_on",
    )(*(pltpu.with_memory_space_constraint(x, pltpu.VMEM) for x in (new_objects, volume)))
    return new_objects[None], volume


def solution(mesh):
    in_specs = (
        P("angle", None, ("tile", "cuts"), None),
        P(),
        P("angle", ("tile", "cuts"), None),
        P("angle", ("tile", "cuts"), None, None),
        P(None, ("angle", "cuts")),
    )
    out_specs = (P("angle", None, ("tile", "cuts"), None), P("tile", ("angle", "cuts")))
    return jax.shard_map(body, mesh=mesh, in_specs=in_specs, out_specs=out_specs, check_vma=False)
```
